128 devices in a mesh: heads: 4 (over x), ctx: 32 (over y, z, core).
Axes of the slice: x: 4, y: 4, z: 4, core: 2. Of those that a mesh axis runs over, the one named last changes fastest.
Arguments:
- queries: bfloat16 [32, 64, 4096], P('ctx', 'heads'), may hold values from -6 to 6
- keys: bfloat16 [32, 512, 4096], P('ctx', None, 'heads'), may hold values from -6 to 6
- values: bfloat16 [32, 512, 4096], P('ctx', None, 'heads'), may hold values from -16 to 16
- picks: int32 [32, 18], replicated, may hold values from -1 to 31, as said below
- d_out: bfloat16 [32, 64, 4096], P('ctx', 'heads'), may hold values from -16 to 16
Outputs:
- out: bfloat16 [32, 64, 4096], P('ctx', 'heads')
- d_queries: bfloat16 [32, 64, 4096], P('ctx', 'heads')
- d_keys: bfloat16 [32, 512, 4096], P('ctx', None, 'heads')
- d_values: bfloat16 [32, 512, 4096], P('ctx', None, 'heads')
The draws below stay inside these ranges and needn't reach their ends.
Inputs may be any that keep to these rules, and one draw needn't show every extreme that they name: `picks`: entry 0 of row b is b; entries 1 to min(b, 17) name distinct blocks before b; the remaining entries are -1.
All inputs are finite; a program needn't handle non-finite values.
Results may differ from the reference program's by a relative error of at most 0.029.
Values may be sent and summed in bfloat16 or wider, within the bound.
A program may use at most 128 MiB of HBM per device.

```python
import math
import jax
import jax.numpy as jnp
from jax import lax

DH = 128
HEADS_DEV = 8
HEADS = 32
BLOCK = 512
NBLK = 32
QROWS = 64
TOPK = 18
N_HEADS = 4


def draw_queries(key, part):
    key = jax.random.fold_in(key, 21)
    first = jax.random.fold_in(key, 0)
    array_shape = (NBLK, QROWS, HEADS * DH)
    return jnp.clip(1.5 * jax.random.normal(first, array_shape, jnp.float32), -6.0, 6.0).astype(jnp.bfloat16)


def draw_keys(key, part):
    key = jax.random.fold_in(key, 22)
    first = jax.random.fold_in(key, 0)
    array_shape = (NBLK, BLOCK, HEADS * DH)
    return jnp.clip(jax.random.normal(first, array_shape, jnp.float32), -6.0, 6.0).astype(jnp.bfloat16)


def draw_picks(key, part):
    key = jax.random.fold_in(key, 7)
    later = jnp.arange(NBLK, dtype=jnp.int32)[:, None]
    earlier = jnp.arange(NBLK, dtype=jnp.int32)[None, :]
    priority = jax.random.randint(key, (NBLK, NBLK), 0, 1048576) * NBLK + earlier
    ranked = jnp.where(earlier < later, priority, -1)
    values_top, index_top = lax.top_k(ranked, TOPK - 1)
    picked = jnp.where(values_top >= 0, index_top, -1).astype(jnp.int32)
    return jnp.concatenate([later, picked], axis=1)


def steps_of(rng, extent, shards, smallest, high):
    gain, own = 1.0, jax.random.fold_in(rng, 6)
    for axis_at, blocks in shards:
        heights = jnp.exp(jax.random.uniform(jax.random.fold_in(own, axis_at), (blocks,), jnp.float32, smallest / len(shards), high / len(shards)))
        gain = gain * jnp.repeat(heights, extent[axis_at] // blocks).reshape([-1 if axis == axis_at else 1 for axis in range(len(extent))])
    return gain


def gaussian(rng, dims, deviation, limit, pieces=(), kind=jnp.bfloat16):
    drawn = deviation * jax.random.normal(rng, dims, jnp.float32)
    if pieces:
        drawn = drawn * steps_of(rng, dims, pieces, -0.22, 0.18)
    return jnp.clip(drawn, -limit, limit).astype(kind)


def setup_inputs(seed: int = 0) -> dict:
    splits = jax.random.split(jax.random.key(seed), 6)
    return {
        "queries": draw_queries(jax.random.fold_in(splits[5], 71), 0),
        "keys": draw_keys(jax.random.fold_in(splits[5], 71), 0),
        "values": gaussian(splits[2], (NBLK, BLOCK, HEADS * DH), 4.0, 16.0, ((0, 32), (2, 4))),
        "picks": draw_picks(jax.random.fold_in(splits[5], 71), 0),
        "d_out": gaussian(splits[4], (NBLK, QROWS, HEADS * DH), 4.0, 16.0, ((0, 32), (1, 4))),
    }


big_negative = -1e+30

def to_half(wide_values):
    rounded = wide_values.astype(jnp.bfloat16)
    return lax.optimization_barrier(rounded).astype(jnp.float32)

def reference(queries, keys, values, picks, d_out):
    inv_root = 1.0 / math.sqrt(DH)
    group_width = HEADS_DEV * DH
    query_pos = BLOCK - QROWS + jnp.arange(QROWS, dtype=jnp.int32)[:, None]
    key_pos = jnp.arange(BLOCK, dtype=jnp.int32)[None, :]
    causal = key_pos <= query_pos
    out_groups = []
    dq_groups = []
    dk_groups = []
    dv_groups = []
    for head_group in range(N_HEADS):
        first_col = head_group * group_width
        query_all = queries[:, :, first_col:first_col + group_width]
        key_all = keys[:, :, first_col:first_col + group_width]
        value_all = values[:, :, first_col:first_col + group_width]
        grad_all = d_out[:, :, first_col:first_col + group_width]

        def one_block(carried, inputs):
            dk_acc, dv_acc = carried
            block_index, query_block, grad_block, chosen = inputs
            usable = chosen >= 0
            where_at = jnp.maximum(chosen, 0).astype(jnp.int32)
            key_sel = key_all[where_at].reshape(TOPK, BLOCK, HEADS_DEV, DH).astype(jnp.float32)
            value_sel = value_all[where_at].reshape(TOPK, BLOCK, HEADS_DEV, DH).astype(jnp.float32)
            query_wide = query_block.reshape(QROWS, HEADS_DEV, DH).astype(jnp.float32)
            grad_wide = grad_block.reshape(QROWS, HEADS_DEV, DH).astype(jnp.float32)
            scores = jnp.einsum('qhd,tkhd->thqk', query_wide, key_sel) * inv_root
            is_own = (chosen == block_index)[:, None, None, None]
            allowed = jnp.logical_and(usable[:, None, None, None], jnp.logical_or(jnp.logical_not(is_own), causal[None, None]))
            scores = jnp.where(allowed, scores, big_negative)
            row_peak = lax.optimization_barrier(jnp.max(scores, axis=3, keepdims=True))
            weights = jnp.exp(scores - row_peak)
            row_total = lax.optimization_barrier(jnp.sum(weights, axis=3, keepdims=True))
            blended = jnp.einsum('thqk,tkhd->tqhd', to_half(weights), value_sel)
            partials = to_half(blended / jnp.transpose(row_total, (0, 2, 1, 3)))
            part_level = jnp.where(usable[:, None, None], (row_peak + jnp.log(row_total))[..., 0], big_negative)
            highest = lax.optimization_barrier(jnp.max(part_level, axis=0))
            level_all = highest + jnp.log(lax.optimization_barrier(jnp.sum(jnp.exp(part_level - highest), axis=0)))
            shares = jnp.exp(part_level - level_all)
            merged = lax.optimization_barrier(jnp.sum(jnp.transpose(shares, (0, 2, 1))[..., None] * partials, axis=0))
            out_wide = to_half(merged)
            out_block = out_wide.astype(jnp.bfloat16)
            deltas = lax.optimization_barrier(jnp.sum(grad_wide * out_wide, axis=2))
            prob_tile = jnp.where(allowed, jnp.exp(scores - level_all[None, :, :, None]), 0.0)
            dprob_tile = jnp.einsum('qhd,tkhd->thqk', grad_wide, value_sel)
            dscores = to_half(prob_tile * (dprob_tile - jnp.transpose(deltas)[None, :, :, None]))
            dv_terms = jnp.einsum('thqk,qhd->tkhd', to_half(prob_tile), grad_wide)
            dk_terms = jnp.einsum('thqk,qhd->tkhd', dscores, query_wide) * inv_root
            dq_terms = to_half(jnp.einsum('thqk,tkhd->tqhd', dscores, key_sel) * inv_root)
            dq_terms = jnp.where(usable[:, None, None, None], dq_terms, 0.0)
            dq_block = lax.optimization_barrier(jnp.sum(dq_terms, axis=0)).astype(jnp.bfloat16)
            dk_acc = dk_acc.at[where_at].add(dk_terms.reshape(TOPK, BLOCK, group_width))
            dv_acc = dv_acc.at[where_at].add(dv_terms.reshape(TOPK, BLOCK, group_width))
            return ((dk_acc, dv_acc), (out_block.reshape(QROWS, group_width), dq_block.reshape(QROWS, group_width)))
        initial = (jnp.zeros((NBLK, BLOCK, group_width), jnp.float32), jnp.zeros((NBLK, BLOCK, group_width), jnp.float32))
        block_ids = jnp.arange(NBLK, dtype=jnp.int32)
        (dk_acc, dv_acc), (out_group, dq_group) = lax.scan(one_block, initial, (block_ids, query_all, grad_all, picks))
        out_groups.append(out_group)
        dq_groups.append(dq_group)
        dk_groups.append(dk_acc.astype(jnp.bfloat16))
        dv_groups.append(dv_acc.astype(jnp.bfloat16))
    out = jnp.concatenate(out_groups, axis=2)
    d_queries = jnp.concatenate(dq_groups, axis=2)
    d_keys = jnp.concatenate(dk_groups, axis=2)
    d_values = jnp.concatenate(dv_groups, axis=2)
    return (out, d_queries, d_keys, d_values)
```

```python
import functools
import math

import jax
import jax.numpy as jnp
from jax import lax
from jax.experimental import pallas as pl
from jax.experimental.pallas import tpu as pltpu
from jax.sharding import PartitionSpec as P

MESH = pl.DeviceIdType.MESH
DH = 128
HEADS_DEV = 8
BLOCK = 512
NBLK = 32
ROWS = 64
WIDTH = HEADS_DEV * DH
HALF = WIDTH // 2
HALF_HEADS = HEADS_DEV // 2
LINE = 8 * ROWS
SCALE = 1.0 / math.sqrt(DH)
SCALE2 = SCALE * math.log2(math.e)
BIG = 1e30
f32 = jnp.float32
bf16 = jnp.bfloat16

NT = (((1,), (1,)), ((), ()))
NN = (((1,), (0,)), ((), ()))
TN = (((0,), (0,)), ((), ()))


def dot(a, b, dims):
    return lax.dot_general(a, b, dims, preferred_element_type=f32)


def add(*parts):
    total = parts[0].astype(f32)
    for part in parts[1:]:
        total = total + part.astype(f32)
    return total.astype(bf16)


def place():
    x = lax.axis_index("heads")
    ctx = lax.axis_index("ctx")
    return x, ctx // 8, lax.rem(ctx // 2, 4), lax.rem(ctx, 2)


def ctx_id(y, z, core):
    return (y * 4 + z) * 2 + core


def remote(src, dst, send, recv, device):
    return pltpu.make_async_remote_copy(
        src_ref=src, dst_ref=dst, send_sem=send, recv_sem=recv, device_id=device, device_id_type=MESH
    )


def meet():
    x, me = lax.axis_index("heads"), lax.axis_index("ctx")
    barrier = pltpu.get_barrier_semaphore()
    for d in (1, 2, 3):
        pl.semaphore_signal(barrier, inc=1, device_id={"heads": lax.rem(x + d, 4)}, device_id_type=MESH)

    def greet(d, carry):
        pl.semaphore_signal(barrier, inc=1, device_id={"ctx": lax.rem(me + d, NBLK)}, device_id_type=MESH)
        return carry

    lax.fori_loop(1, NBLK, greet, 0)
    pl.semaphore_wait(barrier, NBLK - 1 + 3)


class Ring:
    def __init__(self, half):
        x, y, z, core = place()
        self.half, self.core = half, core
        self.cols = pl.ds(half * HALF, HALF)
        self.a, self.b = (y, z) if half == 0 else (z, y)
        self.s = 1 - 2 * core

    def at_a(self, d):
        return lax.rem(self.a + d + 4, 4)

    def at_b(self, d):
        return lax.rem(self.b + d + 4, 4)

    def device(self, da, db):
        a, b = self.at_a(da), self.at_b(db)
        y, z = (a, b) if self.half == 0 else (b, a)
        return {"ctx": ctx_id(y, z, self.core)}

    def sibling(self):
        y, z = (self.a, self.b) if self.half == 0 else (self.b, self.a)
        return {"ctx": ctx_id(y, z, 1 - self.core)}

    def block(self, ref, a, b):
        y, z = (a, b) if self.half == 0 else (b, a)
        return ref.at[y, z, self.core, :, self.cols]

    def line(self, ref, b, core):
        return ref.at[:, b, core, :, self.cols] if self.half == 0 else ref.at[b, :, core, :, self.cols]

    def line4(self, ref, b):
        return ref.at[:, b, :, self.cols] if self.half == 0 else ref.at[b, :, :, self.cols]


class Mover:
    def __init__(self, send, recv):
        self.send, self.recv = send, recv
        self.rings = [Ring(0), Ring(1)]
        self.sent = []

    def go(self, half, n, src, dst, device):
        copy = remote(src, dst, self.send.at[half, n], self.recv.at[half, n], device)
        copy.start()
        self.sent.append(copy)

    def got(self, half, n, ref):
        remote(ref, ref, self.send.at[half, n], self.recv.at[half, n], self.rings[half].sibling()).wait_recv()

    def flush(self):
        for copy in self.sent:
            copy.wait_send()


class Gather(Mover):
    def __init__(self, out, send, recv):
        super().__init__(send, recv)
        self.out = out

    def pass_on(self, half, n, ref, device):
        self.go(half, n, ref, ref, device)

    def a_near(self):
        for h, g in enumerate(self.rings):
            own = g.block(self.out, g.a, g.b)
            self.pass_on(h, 0, own, g.device(g.s, 0))
            self.pass_on(h, 1, own, g.device(-g.s, 0))

    def a_far(self):
        for h, g in enumerate(self.rings):
            block = g.block(self.out, g.at_a(-g.s), g.b)
            self.got(h, 0, block)
            self.pass_on(h, 2, block, g.device(g.s, 0))

    def a_done(self):
        for h, g in enumerate(self.rings):
            self.got(h, 1, g.block(self.out, g.at_a(g.s), g.b))
            self.got(h, 2, g.block(self.out, g.at_a(2), g.b))

    def to_sibling(self, h, n, b):
        g = self.rings[h]
        self.pass_on(h, 6 + n, g.line(self.out, b, g.core), g.sibling())

    def b_near(self):
        for h, g in enumerate(self.rings):
            line = g.line(self.out, g.b, g.core)
            self.pass_on(h, 3, line, g.device(0, g.s))
            self.pass_on(h, 4, line, g.device(0, -g.s))
            self.to_sibling(h, 0, g.b)

    def b_far(self):
        for h, g in enumerate(self.rings):
            b = g.at_b(-g.s)
            line = g.line(self.out, b, g.core)
            self.got(h, 3, line)
            self.pass_on(h, 5, line, g.device(0, g.s))
            self.to_sibling(h, 1, b)

    def b_mid(self):
        for h, g in enumerate(self.rings):
            b = g.at_b(g.s)
            self.got(h, 4, g.line(self.out, b, g.core))
            self.to_sibling(h, 2, b)

    def b_done(self):
        for h, g in enumerate(self.rings):
            b = g.at_b(2)
            self.got(h, 5, g.line(self.out, b, g.core))
            self.to_sibling(h, 3, b)

    def from_sibling(self, n):
        for h, g in enumerate(self.rings):
            b = [g.b, g.at_b(g.s), g.at_b(-g.s), g.at_b(2)][n]
            self.got(h, 6 + n, g.line(self.out, b, 1 - g.core))


class Scatter(Mover):
    def __init__(self, terms, sib, far_b, near_b, far_a, near_a, send, recv):
        super().__init__(send, recv)
        self.terms, self.sib = terms, sib
        self.far_b, self.near_b, self.far_a, self.near_a = far_b, near_b, far_a, near_a

    def to_sibling(self, h, n):
        g = self.rings[h]
        b = [g.at_b(2), g.at_b(g.s), g.at_b(-g.s), g.b][n]
        self.go(h, n, g.line(self.terms, b, 1 - g.core), g.line4(self.sib, b), g.sibling())

    def add_sibling(self, h, n):
        g = self.rings[h]
        b = [g.at_b(2), g.at_b(-g.s), g.at_b(g.s), g.b][n]
        other = g.line4(self.sib, b)
        self.got(h, n, other)
        mine = g.line(self.terms, b, g.core)
        mine[...] = add(mine[...], other[...])

    def b_far(self):
        for h, g in enumerate(self.rings):
            self.add_sibling(h, 0)
            self.go(h, 4, g.line(self.terms, g.at_b(2), g.core), self.far_b.at[h], g.device(0, g.s))

    def b_near(self):
        for h, g in enumerate(self.rings):
            self.add_sibling(h, 1)
            self.go(h, 5, g.line(self.terms, g.at_b(-g.s), g.core), self.near_b.at[h, 0], g.device(0, -g.s))

    def b_turn(self):
        for h, g in enumerate(self.rings):
            self.add_sibling(h, 2)
            self.got(h, 4, self.far_b.at[h])
            line = g.line(self.terms, g.at_b(g.s), g.core)
            line[...] = add(line[...], self.far_b[h])
            self.go(h, 6, line, self.near_b.at[h, 1], g.device(0, g.s))

    def b_end(self):
        for h, g in enumerate(self.rings):
            self.add_sibling(h, 3)
            self.got(h, 5, self.near_b.at[h, 0])
            self.got(h, 6, self.near_b.at[h, 1])
            line = g.line(self.terms, g.b, g.core)
            line[...] = add(line[...], self.near_b[h, 0], self.near_b[h, 1])
            self.go(h, 7, g.block(self.terms, g.at_a(2), g.b), self.far_a.at[h], g.device(g.s, 0))
            self.go(h, 8, g.block(self.terms, g.at_a(-g.s), g.b), self.near_a.at[h, 0], g.device(-g.s, 0))

    def a_turn(self):
        for h, g in enumerate(self.rings):
            self.got(h, 7, self.far_a.at[h])
            block = g.block(self.terms, g.at_a(g.s), g.b)
            block[...] = add(block[...], self.far_a[h])
            self.go(h, 9, block, self.near_a.at[h, 1], g.device(g.s, 0))

    def a_end(self):
        for h, g in enumerate(self.rings):
            self.got(h, 8, self.near_a.at[h, 0])
            self.got(h, 9, self.near_a.at[h, 1])
            block = g.block(self.terms, g.a, g.b)
            block[...] = add(block[...], self.near_a[h, 0], self.near_a[h, 1])


class Heads:
    def __init__(self, wide, own, inward, send, recv, local):
        x = lax.axis_index("heads")
        self.x, self.wide, self.own, self.inward, self.send, self.recv = x, wide, own, inward, send, recv
        self.copies = []
        for d in (1, 2, 3):
            to = lax.rem(x + d, 4)
            src, dst = (self.cols(to), self.rows(x)) if inward else (self.rows(to), self.cols(x))
            copy = remote(src, dst, send.at[d - 1], recv.at[d - 1], {"heads": to})
            copy.start()
            self.copies.append(copy)
        src, dst = (self.cols(x), self.rows(x)) if inward else (self.rows(x), self.cols(x))
        self.local = pltpu.make_async_copy(src, dst, local)
        self.local.start()

    def cols(self, x):
        return self.wide.at[:, pl.ds(pl.multiple_of(x * WIDTH, WIDTH), WIDTH)]

    def rows(self, x):
        return self.own.at[pl.ds(pl.multiple_of(x * 16, 16), 16), :]

    def arrived(self):
        self.local.wait()
        for d in (1, 2, 3):
            source = lax.rem(self.x - d + 4, 4)
            dst = self.rows(source) if self.inward else self.cols(source)
            remote(dst, dst, self.send.at[d - 1], self.recv.at[d - 1], {"heads": source}).wait_recv()

    def flush(self):
        for copy in self.copies:
            copy.wait_send()


def all_lanes(shape):
    return lax.broadcasted_iota(jnp.int32, shape, 1)


def fetch(ref, half, b, h):
    cols = pl.ds(h * DH, DH)
    tile = ref[:, b, :, :, cols] if half == 0 else ref[b, :, :, :, cols]
    return tile.reshape(LINE, DH)


def put(ref, half, b, h, tile):
    tile = tile.reshape(4, 2, ROWS, DH)
    cols = pl.ds(h * DH, DH)
    if half == 0:
        ref[:, b, :, :, cols] = tile
    else:
        ref[b, :, :, :, cols] = tile


def forward_line(half, b, q, k, vx, weights, out, peaks, bias):
    lane = all_lanes((LINE, DH))
    stats = jnp.zeros((LINE, DH), f32)
    for h in range(half * HALF_HEADS, (half + 1) * HALF_HEADS):
        scores = dot(fetch(q, half, b, h), k[:, h * DH : (h + 1) * DH], NT)
        late = scores[:, BLOCK - DH :] + bias[half, b]
        scores = jnp.concatenate([scores[:, : BLOCK - DH], late], axis=1)
        peak = jnp.max(scores, axis=1, keepdims=True)
        w = jnp.exp2((scores - peak) * SCALE2).astype(bf16)
        weights[h, b] = w
        both = dot(w, vx[h], NN)
        put(out, half, b, h, both[:, :DH].astype(bf16))
        stats = jnp.where(lane == h, peak * SCALE, stats)
        stats = jnp.where(lane == HEADS_DEV + h, both[:, DH:], stats)
    peaks[half, b] = stats


def backward_line(half, b, q, g, k, v, weights, factors, dq, dk, dv):
    factor = (factors[:, b] if half == 0 else factors[b]).reshape(LINE, DH)
    for h in range(half * HALF_HEADS, (half + 1) * HALF_HEADS):
        cols = slice(h * DH, (h + 1) * DH)
        share, delta = factor[:, h : h + 1], factor[:, HEADS_DEV + h : HEADS_DEV + h + 1]
        grad = (fetch(g, half, b, h).astype(f32) * share).astype(bf16)
        w = weights[h, b]
        dprob = dot(grad, v[:, cols], NT)
        dscores = (w.astype(f32) * (dprob - delta)).astype(bf16)
        dv[:, cols] += dot(w, grad, TN)
        dk[:, cols] += dot(dscores, fetch(q, half, b, h), TN)
        put(dq, half, b, h, (dot(dscores, k[:, cols], NN) * SCALE).astype(bf16))


def kernel(
    q_in, k_in, v_in, picks, g_in,
    out_ref, dq_ref, dk_ref, dv_ref,
    q, g, out, dq, k, v, vx, weights, dk, dv, bias, live, peaks, columns, factors,
    tell, told, merged,
    sib, far_b, near_b, far_a, near_a,
    gather_send, gather_recv, scatter_send, scatter_recv,
    heads_send, heads_recv, heads_local, stat_send, stat_recv, local,
):
    x, y, z, core = place()
    me = lax.axis_index("ctx")
    load_k = pltpu.make_async_copy(k_in, k, local.at[0])
    load_v = pltpu.make_async_copy(v_in, v, local.at[1])
    load_k.start()
    load_v.start()
    meet()
    in_q = Heads(q_in, q.at[y, z, core], True, heads_send.at[0], heads_recv.at[0], heads_local.at[0])
    in_g = Heads(g_in, g.at[y, z, core], True, heads_send.at[1], heads_recv.at[1], heads_local.at[1])
    move_q = Gather(q, gather_send.at[0], gather_recv.at[0])
    move_g = Gather(g, gather_send.at[1], gather_recv.at[1])
    rings = move_q.rings

    load_k.wait()
    load_v.wait()
    for h in range(HEADS_DEV):
        vx[h, :, :DH] = v[:, h * DH : (h + 1) * DH]
        vx[h, :, DH:] = jnp.ones((BLOCK, DH), bf16)
    in_q.arrived()
    move_q.a_near()
    dk[...] = jnp.zeros_like(dk)
    dv[...] = jnp.zeros_like(dv)
    bias[...] = jnp.zeros_like(bias)
    row = lax.broadcasted_iota(jnp.int32, (ROWS, DH), 0)
    late = jnp.where(all_lanes((ROWS, DH)) - (DH - ROWS) > row, -BIG, 0.0)
    for half, r in enumerate(rings):
        bias[half, r.b, pl.ds(pl.multiple_of((r.a * 2 + core) * ROWS, ROWS), ROWS), :] = late
    in_g.arrived()
    move_g.a_near()
    chosen = jnp.max(jnp.where(picks[...] == me, 0.0, -BIG), axis=1, keepdims=True)
    for b in range(NBLK):
        live[b] = jnp.broadcast_to(chosen[b : b + 1, :], (HEADS_DEV, DH))
    move_q.a_far()
    move_q.a_done()
    move_q.b_near()
    move_g.a_far()
    move_g.a_done()

    def forward(half, d):
        forward_line(half, rings[half].at_b(d), q, k, vx, weights, out, peaks, bias)

    s = 1 - 2 * core
    move_q.from_sibling(0)
    forward(0, 0)
    forward(1, 0)
    move_q.b_far()
    move_q.b_mid()
    move_g.b_near()
    move_q.from_sibling(2)
    forward(0, -s)
    forward(1, -s)
    move_q.from_sibling(1)
    move_g.b_far()
    forward(0, s)
    move_g.b_mid()
    forward(1, s)
    move_q.b_done()
    move_q.from_sibling(3)
    forward(0, 2)
    move_g.b_done()
    forward(1, 2)
    for n in range(4):
        move_g.from_sibling(n)

    lane = all_lanes((HEADS_DEV, DH))
    wide_lane = all_lanes((2 * ROWS, DH))

    def tell_chip(i, carry):
        cy, cz = i // 4, lax.rem(i, 4)
        stats = peaks[0, cz, pl.ds(pl.multiple_of(cy * 2 * ROWS, 2 * ROWS), 2 * ROWS), :]
        stats = stats + peaks[1, cy, pl.ds(pl.multiple_of(cz * 2 * ROWS, 2 * ROWS), 2 * ROWS), :]
        for h in range(HEADS_DEV):
            cols = pl.ds(h * DH, DH)
            products = g[cy, cz, :, :, cols].astype(f32) * out[cy, cz, :, :, cols].astype(f32)
            delta = jnp.sum(products.reshape(2 * ROWS, DH), axis=1, keepdims=True)
            stats = jnp.where(wide_lane == 2 * HEADS_DEV + h, delta, stats)
        columns[cy, cz] = stats
        turned = stats.T
        total = turned[HEADS_DEV : 2 * HEADS_DEV]
        alive = jnp.where(lane < ROWS, live[2 * i], live[2 * i + 1])
        level = turned[:HEADS_DEV] + jnp.log(total) + alive
        delta = turned[2 * HEADS_DEV : 3 * HEADS_DEV] / total
        tell[2 * i] = jnp.where(lane < ROWS, level, pltpu.roll(delta, ROWS, 1))
        tell[2 * i + 1] = jnp.where(lane < ROWS, pltpu.roll(level, ROWS, 1), delta)
        for c in range(2):

            @pl.when(2 * i + c != me)
            def _():
                remote(
                    tell.at[2 * i + c], told.at[me], stat_send.at[0, 2 * i + c], stat_recv.at[0, me], {"ctx": 2 * i + c}
                ).start()

        return carry

    lax.fori_loop(0, NBLK // 2, tell_chip, 0)
    told[me] = tell[me]

    def hear(phase, ref):
        def one(d, carry):
            peer = lax.rem(me + d, NBLK)
            remote(
                ref.at[peer], ref.at[peer], stat_send.at[phase, peer], stat_recv.at[phase, peer], {"ctx": peer}
            ).wait_recv()
            return carry

        lax.fori_loop(1, NBLK, one, 0)

    hear(0, told)
    every = told[...]
    highest = jnp.max(every, axis=0)
    grown = jnp.exp(every - highest[None])
    total = jnp.sum(grown, axis=0)
    level = highest + jnp.log(total)
    delta = jnp.zeros((HEADS_DEV, DH), f32)
    for b in range(NBLK):
        delta = delta + pltpu.roll(grown[b], ROWS, 1) * every[b]
    delta = delta / pltpu.roll(total, ROWS, 1)
    merged[me] = jnp.where(lane < ROWS, level, delta)

    def share_level(d, carry):
        peer = lax.rem(me + d, NBLK)
        remote(merged.at[me], merged.at[me], stat_send.at[1, peer], stat_recv.at[1, me], {"ctx": peer}).start()
        return carry

    lax.fori_loop(1, NBLK, share_level, 0)
    hear(1, merged)

    def weigh_chip(i, carry):
        cy, cz = i // 4, lax.rem(i, 4)
        first, second = merged[2 * i], merged[2 * i + 1]
        level = jnp.where(lane < ROWS, first, pltpu.roll(second, ROWS, 1))
        delta = jnp.where(lane < ROWS, pltpu.roll(first, ROWS, 1), second)
        level = level - jnp.where(lane < ROWS, live[2 * i], live[2 * i + 1])
        rows = jnp.concatenate([level, delta, jnp.zeros((DH - 2 * HEADS_DEV, DH), f32)], axis=0)
        turned = rows.T
        share = jnp.exp(columns[cy, cz] - turned)
        share = jnp.where(wide_lane < HEADS_DEV, share, 0.0)
        factors[cy, cz] = jnp.where(wide_lane < HEADS_DEV, share, pltpu.roll(share, HEADS_DEV, 1) * turned)
        for h in range(HEADS_DEV):
            cols = pl.ds(h * DH, DH)
            part = out[cy, cz, :, :, cols].reshape(2 * ROWS, DH).astype(f32) * share[:, h : h + 1]
            out[cy, cz, :, :, cols] = part.astype(bf16).reshape(2, ROWS, DH)
        return carry

    lax.fori_loop(0, NBLK // 2, weigh_chip, 0)

    def scatter(n, terms):
        return Scatter(
            terms, sib.at[n], far_b.at[n], near_b.at[n], far_a.at[n], near_a.at[n], scatter_send.at[n], scatter_recv.at[n]
        )

    sum_out, sum_dq = scatter(0, out), scatter(1, dq)
    for n in range(4):
        for half in (0, 1):
            sum_out.to_sibling(half, n)

    def backward(half, d, n):
        backward_line(half, rings[half].at_b(d), q, g, k, v, weights, factors, dq, dk, dv)
        sum_dq.to_sibling(half, n)

    backward(0, 2, 0)
    sum_out.b_far()
    sum_out.b_near()
    backward(1, 2, 0)
    sum_out.b_turn()
    backward(0, -s, 2)
    sum_out.b_end()
    backward(1, -s, 2)
    sum_dq.b_far()
    sum_out.a_turn()
    backward(0, s, 1)
    backward(1, s, 1)
    sum_dq.b_near()
    sum_out.a_end()
    out_heads = Heads(
        out_ref, out.at[y, z, core], False, heads_send.at[2], heads_recv.at[2], heads_local.at[2]
    )
    backward(0, 0, 3)
    backward(1, 0, 3)
    sum_dq.b_turn()
    for h in range(HEADS_DEV):
        cols = slice(h * DH, (h + 1) * DH)
        k[:, cols] = (dk[:, cols] * SCALE).astype(bf16)
        v[:, cols] = dv[:, cols].astype(bf16)
    save_k = pltpu.make_async_copy(k, dk_ref, local.at[0])
    save_v = pltpu.make_async_copy(v, dv_ref, local.at[1])
    save_k.start()
    save_v.start()
    sum_dq.b_end()
    sum_dq.a_turn()
    sum_dq.a_end()
    dq_heads = Heads(dq_ref, dq.at[y, z, core], False, heads_send.at[3], heads_recv.at[3], heads_local.at[3])
    out_heads.arrived()

    def told_all(d, carry):
        peer = lax.rem(me + d, NBLK)
        remote(tell.at[peer], told.at[me], stat_send.at[0, peer], stat_recv.at[0, me], {"ctx": peer}).wait_send()
        remote(merged.at[me], merged.at[me], stat_send.at[1, peer], stat_recv.at[1, me], {"ctx": peer}).wait_send()
        return carry

    lax.fori_loop(1, NBLK, told_all, 0)
    for mover in (in_q, in_g, move_q, move_g, sum_out, sum_dq, out_heads):
        mover.flush()
    save_k.wait()
    save_v.wait()
    dq_heads.arrived()
    dq_heads.flush()


def body(queries, keys, values, picks, d_out):
    rows, wide = jax.ShapeDtypeStruct((16, 4 * WIDTH), bf16), jax.ShapeDtypeStruct((BLOCK, WIDTH), bf16)
    anywhere, vmem = pl.BlockSpec(memory_space=pl.ANY), pl.BlockSpec(memory_space=pltpu.VMEM)
    windows = pltpu.VMEM((4, 4, 2, ROWS, WIDTH), bf16)
    dma = pltpu.SemaphoreType.DMA
    out, dq, dk, dv = pl.pallas_call(
        kernel,
        out_shape=(rows, rows, wide, wide),
        in_specs=[anywhere, anywhere, anywhere, vmem, anywhere],
        out_specs=[anywhere] * 4,
        scratch_shapes=[
            windows, windows, windows, windows,
            pltpu.VMEM((BLOCK, WIDTH), bf16), pltpu.VMEM((BLOCK, WIDTH), bf16),
            pltpu.VMEM((HEADS_DEV, BLOCK, 2 * DH), bf16),
            pltpu.VMEM((HEADS_DEV, 4, LINE, BLOCK), bf16),
            pltpu.VMEM((BLOCK, WIDTH), f32), pltpu.VMEM((BLOCK, WIDTH), f32),
            pltpu.VMEM((2, 4, LINE, DH), f32),
            pltpu.VMEM((NBLK, HEADS_DEV, DH), f32),
            pltpu.VMEM((2, 4, LINE, DH), f32),
            pltpu.VMEM((4, 4, 2 * ROWS, DH), f32), pltpu.VMEM((4, 4, 2 * ROWS, DH), f32),
            pltpu.VMEM((NBLK, HEADS_DEV, DH), f32), pltpu.VMEM((NBLK, HEADS_DEV, DH), f32),
            pltpu.VMEM((NBLK, HEADS_DEV, DH), f32),
            pltpu.VMEM((2, 4, 4, ROWS, WIDTH), bf16),
            pltpu.VMEM((2, 2, 4, ROWS, HALF), bf16), pltpu.VMEM((2, 2, 2, 4, ROWS, HALF), bf16),
            pltpu.VMEM((2, 2, ROWS, HALF), bf16), pltpu.VMEM((2, 2, 2, ROWS, HALF), bf16),
            dma((2, 2, 10)), dma((2, 2, 10)), dma((2, 2, 10)), dma((2, 2, 10)),
            dma((4, 3)), dma((4, 3)), dma((4,)), dma((2, NBLK)), dma((2, NBLK)), dma((2,)),
        ],
        compiler_params=pltpu.CompilerParams(collective_id=0, has_side_effects=True, vmem_limit_bytes=63 << 20),
        name="block_attention",
    )(queries[0], keys[0], values[0], picks, d_out[0])
    return out[None], dq[None], dk[None], dv[None]


def solution(mesh):
    rows, blocks = P("ctx", "heads", None), P("ctx", None, "heads")
    return jax.shard_map(
        body,
        mesh=mesh,
        in_specs=(rows, blocks, blocks, P(), rows),
        out_specs=(rows, rows, blocks, blocks),
        check_vma=False,
    )
```

```python
import functools
import math

import jax
import jax.numpy as jnp
from jax import lax
from jax.experimental import pallas as pl
from jax.experimental.pallas import tpu as pltpu
from jax.sharding import PartitionSpec as P

MESH = pl.DeviceIdType.MESH
DH = 128
HEADS_DEV = 8
BLOCK = 512
NBLK = 32
ROWS = 64
WIDTH = HEADS_DEV * DH
HALF = WIDTH // 2
QUARTER = WIDTH // 4
LINE = 8 * ROWS
SCALE = 1.0 / math.sqrt(DH)
SCALE2 = SCALE * math.log2(math.e)
BIG = 1e30
f32 = jnp.float32
bf16 = jnp.bfloat16

NT = (((1,), (1,)), ((), ()))
NN = (((1,), (0,)), ((), ()))
TN = (((0,), (0,)), ((), ()))


def dot(a, b, dims):
    return lax.dot_general(a, b, dims, preferred_element_type=f32)


def add(*parts):
    total = parts[0].astype(f32)
    for part in parts[1:]:
        total = total + part.astype(f32)
    return total.astype(bf16)


def place():
    x = lax.axis_index("heads")
    ctx = lax.axis_index("ctx")
    return x, ctx // 8, lax.rem(ctx // 2, 4), lax.rem(ctx, 2)


def ctx_id(y, z, core):
    return (y * 4 + z) * 2 + core


def remote(src, dst, send, recv, device):
    return pltpu.make_async_remote_copy(
        src_ref=src, dst_ref=dst, send_sem=send, recv_sem=recv, device_id=device, device_id_type=MESH
    )


def meet():
    x, me = lax.axis_index("heads"), lax.axis_index("ctx")
    barrier = pltpu.get_barrier_semaphore()
    for d in (1, 2, 3):
        pl.semaphore_signal(barrier, inc=1, device_id={"heads": lax.rem(x + d, 4)}, device_id_type=MESH)

    def greet(d, carry):
        pl.semaphore_signal(barrier, inc=1, device_id={"ctx": lax.rem(me + d, NBLK)}, device_id_type=MESH)
        return carry

    lax.fori_loop(1, NBLK, greet, 0)
    pl.semaphore_wait(barrier, NBLK - 1 + 3)


class Ring:
    def __init__(self, batch, half):
        x, y, z, core = place()
        self.half, self.core = half, core
        self.cols = pl.ds(batch * HALF + half * QUARTER, QUARTER)
        self.heads = range((2 * batch + half) * 2, (2 * batch + half + 1) * 2)
        self.a, self.b = (y, z) if half == 0 else (z, y)
        self.side = 1 - 2 * core

    def at_a(self, d):
        return lax.rem(self.a + d + 4, 4)

    def at_b(self, d):
        return lax.rem(self.b + d + 4, 4)

    def device(self, da, db):
        a, b = self.at_a(da), self.at_b(db)
        y, z = (a, b) if self.half == 0 else (b, a)
        return {"ctx": ctx_id(y, z, self.core)}

    def sibling(self):
        y, z = (self.a, self.b) if self.half == 0 else (self.b, self.a)
        return {"ctx": ctx_id(y, z, 1 - self.core)}

    def block(self, ref, a):
        y, z = (a, self.b) if self.half == 0 else (self.b, a)
        return ref.at[y, z, self.core, :, self.cols]

    def line(self, ref, b, core):
        return ref.at[:, b, core, :, self.cols] if self.half == 0 else ref.at[b, :, core, :, self.cols]

    def bare_line(self, ref, b):
        return ref.at[:, b, :, self.cols] if self.half == 0 else ref.at[b, :, :, self.cols]


class Mover:
    def __init__(self, batch, send, recv):
        self.send, self.recv = send.at[batch], recv.at[batch]
        self.rings = [Ring(batch, 0), Ring(batch, 1)]
        self.sent = []

    def go(self, half, n, src, dst, device):
        copy = remote(src, dst, self.send.at[half, n], self.recv.at[half, n], device)
        copy.start()
        self.sent.append(copy)

    def got(self, half, n, ref):
        remote(ref, ref, self.send.at[half, n], self.recv.at[half, n], self.rings[half].sibling()).wait_recv()

    def flush(self):
        for copy in self.sent:
            copy.wait_send()


class Gather(Mover):
    def __init__(self, batch, out, send, recv):
        super().__init__(batch, send, recv)
        self.out = out

    def a_send(self):
        for h, g in enumerate(self.rings):
            own = g.block(self.out, g.a)
            for d in (1, 3, 2):
                self.go(h, d - 1, own, own, g.device(d, 0))

    def b_send(self):
        for h, g in enumerate(self.rings):
            for d in (1, 3, 2):
                self.got(h, d - 1, g.block(self.out, g.at_a(-d)))
        for h, g in enumerate(self.rings):
            own = g.line(self.out, g.b, g.core)
            for d in (1, 3):
                self.go(h, 2 + d, own, own, g.device(0, d))
            self.go(h, 6, own, own, g.sibling())

    def pass_on(self, d):
        for h, g in enumerate(self.rings):
            line = g.line(self.out, g.at_b(-d), g.core)
            self.got(h, 2 + d, line)
            self.go(h, 6 + d, line, line, g.sibling())

    def pass_far(self):
        for h, g in enumerate(self.rings):
            line = g.line(self.out, g.at_b(-g.side), g.core)
            self.go(h, 4, line, line, g.device(0, g.side))

    def from_sibling(self, d):
        for h, g in enumerate(self.rings):
            self.got(h, 6 + d, g.line(self.out, g.at_b(-d), 1 - g.core))


class Scatter(Mover):
    def __init__(self, batch, terms, sib, lines, blocks, send, recv):
        super().__init__(batch, send, recv)
        self.terms, self.sib, self.lines, self.blocks = terms, sib, lines.at[batch], blocks.at[batch]

    def to_sibling(self, h, d):
        g = self.rings[h]
        b = g.at_b(d)
        self.go(h, d, g.line(self.terms, b, 1 - g.core), g.bare_line(self.sib, b), g.sibling())

    def b_send(self, d):
        for h, g in enumerate(self.rings):
            b = g.at_b(d)
            other = g.bare_line(self.sib, b)
            self.got(h, d, other)
            mine = g.line(self.terms, b, g.core)
            mine[...] = add(mine[...], other[...])
            self.go(h, 3 + d, mine, self.lines.at[h, d - 1], g.device(0, d))

    def a_send(self):
        for h, g in enumerate(self.rings):
            other = g.bare_line(self.sib, g.b)
            self.got(h, 0, other)
            for d in (1, 2, 3):
                self.got(h, 3 + d, self.lines.at[h, d - 1])
            mine = g.line(self.terms, g.b, g.core)
            mine[...] = add(mine[...], other[...], *(self.lines[h, d] for d in range(3)))
            for d in (2, 1, 3):
                self.go(h, 6 + d, g.block(self.terms, g.at_a(d)), self.blocks.at[h, d - 1], g.device(d, 0))

    def finish(self):
        for h, g in enumerate(self.rings):
            for d in (1, 2, 3):
                self.got(h, 6 + d, self.blocks.at[h, d - 1])
            mine = g.block(self.terms, g.a)
            mine[...] = add(mine[...], *(self.blocks[h, d] for d in range(3)))


class Heads:
    def __init__(self, wide, own, inward, send, recv, local):
        x = lax.axis_index("heads")
        self.x, self.wide, self.own, self.inward, self.send, self.recv = x, wide, own, inward, send, recv
        self.copies = []
        for d in (1, 2, 3):
            to = lax.rem(x + d, 4)
            src, dst = (self.cols(to), self.rows(x)) if inward else (self.rows(to), self.cols(x))
            copy = remote(src, dst, send.at[d - 1], recv.at[d - 1], {"heads": to})
            copy.start()
            self.copies.append(copy)
        src, dst = (self.cols(x), self.rows(x)) if inward else (self.rows(x), self.cols(x))
        self.local = pltpu.make_async_copy(src, dst, local)
        self.local.start()

    def cols(self, x):
        return self.wide.at[:, pl.ds(pl.multiple_of(x * WIDTH, WIDTH), WIDTH)]

    def rows(self, x):
        return self.own.at[pl.ds(pl.multiple_of(x * 16, 16), 16), :]

    def arrived(self):
        self.local.wait()
        for d in (1, 2, 3):
            source = lax.rem(self.x - d + 4, 4)
            dst = self.rows(source) if self.inward else self.cols(source)
            remote(dst, dst, self.send.at[d - 1], self.recv.at[d - 1], {"heads": source}).wait_recv()

    def flush(self):
        for copy in self.copies:
            copy.wait_send()


def all_lanes(shape):
    return lax.broadcasted_iota(jnp.int32, shape, 1)


def fetch(ref, half, b, h):
    cols = pl.ds(h * DH, DH)
    tile = ref[:, b, :, :, cols] if half == 0 else ref[b, :, :, :, cols]
    return tile.reshape(LINE, DH)


def put(ref, half, b, h, tile):
    tile = tile.reshape(4, 2, ROWS, DH)
    cols = pl.ds(h * DH, DH)
    if half == 0:
        ref[:, b, :, :, cols] = tile
    else:
        ref[b, :, :, :, cols] = tile


def forward_line(ring, d, q, k, vx, weights, out, peaks, bias, first):
    half, b = ring.half, ring.at_b(-d)
    lane = all_lanes((LINE, DH))
    stats = jnp.zeros((LINE, DH), f32) if first else peaks[half, b]
    for h in ring.heads:
        scores = dot(fetch(q, half, b, h), k[:, h * DH : (h + 1) * DH], NT)
        if d == 0:
            late = scores[:, BLOCK - DH :] + bias[half]
            scores = jnp.concatenate([scores[:, : BLOCK - DH], late], axis=1)
        peak = jnp.max(scores, axis=1, keepdims=True)
        w = jnp.exp2((scores - peak) * SCALE2).astype(bf16)
        weights[h, b] = w
        both = dot(w, vx[h], NN)
        put(out, half, b, h, both[:, :DH].astype(bf16))
        stats = jnp.where(lane == h, peak * SCALE, stats)
        stats = jnp.where(lane == HEADS_DEV + h, both[:, DH:], stats)
    peaks[half, b] = stats


def backward_line(ring, d, q, g, k, v, weights, factors, out, dq, dk, dv):
    half, b = ring.half, ring.at_b(d)
    factor = (factors[:, b] if half == 0 else factors[b]).reshape(LINE, DH)
    for h in ring.heads:
        cols = slice(h * DH, (h + 1) * DH)
        share, delta = factor[:, h : h + 1], factor[:, HEADS_DEV + h : HEADS_DEV + h + 1]
        grad = (fetch(g, half, b, h).astype(f32) * share).astype(bf16)
        put(out, half, b, h, (fetch(out, half, b, h).astype(f32) * share).astype(bf16))
        w = weights[h, b]
        dprob = dot(grad, v[:, cols], NT)
        dscores = (w.astype(f32) * (dprob - delta)).astype(bf16)
        dv[:, cols] += dot(w, grad, TN)
        dk[:, cols] += dot(dscores, fetch(q, half, b, h), TN)
        put(dq, half, b, h, (dot(dscores, k[:, cols], NN) * SCALE).astype(bf16))


def kernel(
    q_in, k_in, v_in, picks_in, g_in,
    out_ref, dq_ref, dk_ref, dv_ref,
    q, g, out, dq, k, v, picks, vx, weights, dk, dv, bias, live, peaks, own_peaks, factors, pick_head,
    tell, told, merged,
    sib, lines, blocks,
    gather_send, gather_recv, scatter_send, scatter_recv,
    heads_send, heads_recv, heads_local, stat_send, stat_recv, local,
):
    x, y, z, core = place()
    me = lax.axis_index("ctx")
    out_ref, dq_ref, dk_ref, dv_ref = out_ref.at[0], dq_ref.at[0], dk_ref.at[0], dv_ref.at[0]
    loads = [pltpu.make_async_copy(a, b, local.at[i]) for i, (a, b) in enumerate([(k_in, k), (v_in, v), (picks_in, picks)])]
    for load in loads:
        load.start()
    meet()
    in_q = Heads(q_in, q.at[y, z, core], True, heads_send.at[0], heads_recv.at[0], heads_local.at[0])
    in_g = Heads(g_in, g.at[y, z, core], True, heads_send.at[1], heads_recv.at[1], heads_local.at[1])
    move_q = [Gather(p, q, gather_send.at[0], gather_recv.at[0]) for p in (0, 1)]
    move_g = [Gather(p, g, gather_send.at[1], gather_recv.at[1]) for p in (0, 1)]
    sum_out, sum_dq = (
        [
            Scatter(p, terms, sib.at[n], lines.at[n], blocks.at[n], scatter_send.at[n], scatter_recv.at[n])
            for p in (0, 1)
        ]
        for n, terms in enumerate((out, dq))
    )
    rings = [move_q[p].rings for p in (0, 1)]
    lane = all_lanes((HEADS_DEV, DH))

    def forward(p, d):
        for ring in rings[p]:
            forward_line(ring, d, q, k, vx, weights, out, peaks, bias, p == 0)

    def tell_levels(p):
        active = lax.broadcasted_iota(jnp.int32, (HEADS_DEV, DH), 0) // 4 == p

        def tell_chip(i, carry):
            cy, cz = i // 4, lax.rem(i, 4)
            stats = peaks[0, cz, pl.ds(pl.multiple_of(cy * 2 * ROWS, 2 * ROWS), 2 * ROWS), :]
            stats = stats + peaks[1, cy, pl.ds(pl.multiple_of(cz * 2 * ROWS, 2 * ROWS), 2 * ROWS), :]
            cols = pl.ds(p * HALF, HALF)
            products = (g[cy, cz, :, :, cols].astype(f32) * out[cy, cz, :, :, cols].astype(f32)).reshape(2 * ROWS, HALF)
            high = products.astype(bf16)
            low = (products - high.astype(f32)).astype(bf16)
            turned = (stats + dot(high, pick_head[p], NN) + dot(low, pick_head[p], NN)).T
            total = jnp.where(active, turned[HEADS_DEV : 2 * HEADS_DEV], 1.0)
            peak = turned[:HEADS_DEV] + jnp.where(lane < ROWS, live[2 * i], live[2 * i + 1])
            own_peaks[p, i] = peak
            level = peak + jnp.log(total)
            delta = turned[2 * HEADS_DEV : 3 * HEADS_DEV] / total
            tell[p, 2 * i] = jnp.where(lane < ROWS, level, pltpu.roll(delta, ROWS, 1))
            tell[p, 2 * i + 1] = jnp.where(lane < ROWS, pltpu.roll(level, ROWS, 1), delta)
            return carry

        lax.fori_loop(0, NBLK // 2, tell_chip, 0, unroll=4)

        def send_level(d, carry):
            peer = lax.rem(me + d, NBLK)
            remote(
                tell.at[p, peer], told.at[p, me], stat_send.at[p, 0, peer], stat_recv.at[p, 0, me], {"ctx": peer}
            ).start()
            return carry

        lax.fori_loop(1, NBLK, send_level, 0)
        told[p, me] = tell[p, me]

    def hear(p, phase, ref):
        def one(d, carry):
            peer = lax.rem(me + d, NBLK)
            row = ref.at[p, peer]
            remote(row, row, stat_send.at[p, phase, peer], stat_recv.at[p, phase, peer], {"ctx": peer}).wait_recv()
            return carry

        lax.fori_loop(1, NBLK, one, 0)

    def merge_levels(p):
        hear(p, 0, told)
        every = told[p]
        highest = jnp.max(every, axis=0)
        grown = jnp.exp(every - highest[None])
        total = jnp.sum(grown, axis=0)
        level = highest + jnp.log(total)
        delta = jnp.zeros((HEADS_DEV, DH), f32)
        for b in range(NBLK):
            delta = delta + pltpu.roll(grown[b], ROWS, 1) * every[b]
        delta = delta / pltpu.roll(total, ROWS, 1)
        merged[p, me] = jnp.where(lane < ROWS, level, delta)
        mine = merged.at[p, me]

        def share_level(d, carry):
            peer = lax.rem(me + d, NBLK)
            remote(mine, mine, stat_send.at[p, 1, peer], stat_recv.at[p, 1, me], {"ctx": peer}).start()
            return carry

        lax.fori_loop(1, NBLK, share_level, 0)

    def weigh(p):
        hear(p, 1, merged)

        def weigh_chip(i, carry):
            first, second = merged[p, 2 * i], merged[p, 2 * i + 1]
            level = jnp.where(lane < ROWS, first, pltpu.roll(second, ROWS, 1))
            delta = jnp.where(lane < ROWS, pltpu.roll(first, ROWS, 1), second)
            share = jnp.exp(own_peaks[p, i] - level)
            rows = jnp.concatenate([share, share * delta], axis=0)
            factors[p, i // 4, lax.rem(i, 4), :, : 2 * HEADS_DEV] = rows.T
            return carry

        lax.fori_loop(0, NBLK // 2, weigh_chip, 0, unroll=4)

    def backward(p, d):
        for half, ring in enumerate(rings[p]):
            backward_line(ring, d, q, g, k, v, weights, factors.at[p], out, dq, dk, dv)
            sum_out[p].to_sibling(half, d)
            sum_dq[p].to_sibling(half, d)

    def b_send(p, d):
        sum_out[p].b_send(d)
        sum_dq[p].b_send(d)

    def a_send(p):
        sum_out[p].a_send()
        sum_dq[p].a_send()

    def finish(p):
        sum_out[p].finish()
        sum_dq[p].finish()

    saves = []

    def save(p):
        for h in range(4 * p, 4 * p + 4):
            cols = slice(h * DH, (h + 1) * DH)
            k[:, cols] = (dk[:, cols] * SCALE).astype(bf16)
            v[:, cols] = dv[:, cols].astype(bf16)
        cols = pl.ds(p * HALF, HALF)
        for n, (src, dst) in enumerate([(k, dk_ref), (v, dv_ref)]):
            saves.append(pltpu.make_async_copy(src.at[:, cols], dst.at[:, cols], local.at[2 * p + n]))
            saves[-1].start()

    for load in loads:
        load.wait()
    for h in range(HEADS_DEV):
        vx[h, :, :DH] = v[:, h * DH : (h + 1) * DH]
        vx[h, :, DH:] = jnp.ones((BLOCK, DH), bf16)
    in_q.arrived()
    move_q[0].a_send()
    bias[...] = jnp.zeros_like(bias)
    row = lax.broadcasted_iota(jnp.int32, (ROWS, DH), 0)
    late = jnp.where(all_lanes((ROWS, DH)) - (DH - ROWS) > row, -BIG, 0.0)
    for half, r in enumerate(rings[0]):
        bias[half, pl.ds(pl.multiple_of((r.a * 2 + core) * ROWS, ROWS), ROWS), :] = late
    in_g.arrived()
    move_g[0].a_send()
    col = lax.broadcasted_iota(jnp.int32, (HALF, DH), 0) // DH
    for p in (0, 1):
        pick_head[p] = jnp.where(all_lanes((HALF, DH)) == col + 2 * HEADS_DEV + 4 * p, 1.0, 0.0).astype(bf16)
    dk[...] = jnp.zeros_like(dk)
    dv[...] = jnp.zeros_like(dv)
    chosen = jnp.max(jnp.where(picks[...] == me, 0.0, -BIG), axis=0, keepdims=True)
    for b in range(NBLK):
        live[b] = jnp.broadcast_to(chosen[:, b : b + 1], (HEADS_DEV, DH))
    move_q[0].b_send()
    move_q[1].a_send()
    move_g[0].b_send()
    move_g[1].a_send()
    move_q[0].from_sibling(0)
    forward(0, 0)
    move_q[0].pass_on(1)
    move_q[0].pass_on(3)
    move_q[0].pass_far()
    move_q[1].b_send()
    move_q[0].from_sibling(1)
    move_q[0].from_sibling(3)
    forward(0, 1)
    move_g[0].pass_on(1)
    move_g[0].pass_on(3)
    move_g[0].pass_far()
    forward(0, 3)
    move_g[1].b_send()
    move_q[0].pass_on(2)
    move_q[1].from_sibling(0)
    forward(1, 0)
    move_q[1].pass_on(1)
    move_q[1].pass_on(3)
    move_q[1].pass_far()
    move_q[0].from_sibling(2)
    forward(0, 2)
    move_g[0].pass_on(2)
    move_g[1].pass_on(1)
    move_g[1].pass_on(3)
    move_g[1].pass_far()
    move_q[1].from_sibling(1)
    forward(1, 1)
    for d in range(4):
        move_g[0].from_sibling(d)
    tell_levels(0)
    move_q[1].pass_on(2)
    move_q[1].from_sibling(3)
    forward(1, 3)
    move_g[1].pass_on(2)
    merge_levels(0)
    move_q[1].from_sibling(2)
    forward(1, 2)
    for d in range(4):
        move_g[1].from_sibling(d)
    tell_levels(1)
    weigh(0)

    backward(0, 2)
    merge_levels(1)
    backward(0, 1)
    b_send(0, 2)
    backward(0, 3)
    b_send(0, 1)
    weigh(1)
    backward(0, 0)
    b_send(0, 3)
    save(0)
    backward(1, 2)
    a_send(0)
    backward(1, 1)
    b_send(1, 2)
    finish(0)
    backward(1, 3)
    b_send(1, 1)
    backward(1, 0)
    b_send(1, 3)
    save(1)
    a_send(1)
    sum_out[1].finish()
    out_heads = Heads(
        out_ref, out.at[y, z, core], False, heads_send.at[2], heads_recv.at[2], heads_local.at[2]
    )
    sum_dq[1].finish()
    dq_heads = Heads(dq_ref, dq.at[y, z, core], False, heads_send.at[3], heads_recv.at[3], heads_local.at[3])
    out_heads.arrived()

    def told_all(d, carry):
        peer = lax.rem(me + d, NBLK)
        for p in (0, 1):
            mine = merged.at[p, me]
            remote(tell.at[p, peer], told.at[p, me], stat_send.at[p, 0, peer], stat_recv.at[p, 0, me], {"ctx": peer}).wait_send()
            remote(mine, mine, stat_send.at[p, 1, peer], stat_recv.at[p, 1, me], {"ctx": peer}).wait_send()
        return carry

    lax.fori_loop(1, NBLK, told_all, 0)
    for mover in (in_q, in_g, *move_q, *move_g, *sum_out, *sum_dq, out_heads):
        mover.flush()
    for copy in saves:
        copy.wait()
    dq_heads.arrived()
    dq_heads.flush()


def hand_out(*refs):
    copies = [pltpu.make_async_copy(refs[i], refs[4 + i], refs[8].at[i]) for i in range(4)]
    for copy in copies:
        copy.start()
    for copy in copies:
        copy.wait()


def body(queries, keys, values, picks, d_out):
    rows, wide = jax.ShapeDtypeStruct((1, 16, 4 * WIDTH), bf16), jax.ShapeDtypeStruct((1, BLOCK, WIDTH), bf16)
    anywhere = pl.BlockSpec(memory_space=pl.ANY)
    windows = pltpu.VMEM((4, 4, 2, ROWS, WIDTH), bf16)
    levels = pltpu.VMEM((2, NBLK, HEADS_DEV, DH), f32)
    dma = pltpu.SemaphoreType.DMA
    out, dq, dk, dv = pl.pallas_call(
        kernel,
        out_shape=(rows, rows, wide, wide),
        in_specs=[anywhere] * 5,
        out_specs=[anywhere] * 4,
        scratch_shapes=[
            windows, windows, windows, windows,
            pltpu.VMEM((BLOCK, WIDTH), bf16), pltpu.VMEM((BLOCK, WIDTH), bf16),
            pltpu.VMEM(picks.shape[::-1], jnp.int32),
            pltpu.VMEM((HEADS_DEV, BLOCK, 2 * DH), bf16),
            pltpu.VMEM((HEADS_DEV, 4, LINE, BLOCK), bf16),
            pltpu.VMEM((BLOCK, WIDTH), f32), pltpu.VMEM((BLOCK, WIDTH), f32),
            pltpu.VMEM((2, LINE, DH), f32),
            pltpu.VMEM((NBLK, HEADS_DEV, DH), f32),
            pltpu.VMEM((2, 4, LINE, DH), f32),
            pltpu.VMEM((2, NBLK // 2, HEADS_DEV, DH), f32), pltpu.VMEM((2, 4, 4, 2 * ROWS, DH), f32),
            pltpu.VMEM((2, HALF, DH), bf16),
            levels, levels, levels,
            pltpu.VMEM((2, 4, 4, ROWS, WIDTH), bf16),
            pltpu.VMEM((2, 2, 2, 3, 4, ROWS, QUARTER), bf16), pltpu.VMEM((2, 2, 2, 3, ROWS, QUARTER), bf16),
            dma((2, 2, 2, 10)), dma((2, 2, 2, 10)), dma((2, 2, 2, 10)), dma((2, 2, 2, 10)),
            dma((4, 3)), dma((4, 3)), dma((4,)), dma((2, 2, NBLK)), dma((2, 2, NBLK)), dma((4,)),
        ],
        compiler_params=pltpu.CompilerParams(collective_id=0, has_side_effects=True, vmem_limit_bytes=63 << 20),
        name="block_attention",
    )(queries[0], keys[0], values[0], picks.T, d_out[0])
    return pl.pallas_call(
        hand_out,
        out_shape=(out, dq, dk, dv),
        in_specs=[pl.BlockSpec(memory_space=pltpu.VMEM)] * 4,
        out_specs=[anywhere] * 4,
        scratch_shapes=[dma((4,))],
        name="hand_out",
    )(out, dq, dk, dv)


def solution(mesh):
    rows, blocks = P("ctx", "heads", None), P("ctx", None, "heads")
    return jax.shard_map(
        body,
        mesh=mesh,
        in_specs=(rows, blocks, blocks, P(), rows),
        out_specs=(rows, rows, blocks, blocks),
        check_vma=False,
    )
```

```python
import functools
import math

import jax
import jax.numpy as jnp
from jax import lax
from jax.experimental import pallas as pl
from jax.experimental.pallas import tpu as pltpu
from jax.sharding import PartitionSpec as P

MESH = pl.DeviceIdType.MESH
DH = 128
HEADS_DEV = 8
BLOCK = 512
NBLK = 32
ROWS = 64
WIDTH = HEADS_DEV * DH
HALF = WIDTH // 2
QUARTER = WIDTH // 4
LINE = 8 * ROWS
SCALE = 1.0 / math.sqrt(DH)
SCALE2 = SCALE * math.log2(math.e)
BIG = 1e30
f32 = jnp.float32
bf16 = jnp.bfloat16

NT = (((1,), (1,)), ((), ()))
NN = (((1,), (0,)), ((), ()))
TN = (((0,), (0,)), ((), ()))


def dot(a, b, dims):
    return lax.dot_general(a, b, dims, preferred_element_type=f32)


def add(*parts):
    total = parts[0].astype(f32)
    for part in parts[1:]:
        total = total + part.astype(f32)
    return total.astype(bf16)


def place():
    x = lax.axis_index("heads")
    ctx = lax.axis_index("ctx")
    return x, ctx // 8, lax.rem(ctx // 2, 4), lax.rem(ctx, 2)


def ctx_id(y, z, core):
    return (y * 4 + z) * 2 + core


def remote(src, dst, send, recv, device):
    return pltpu.make_async_remote_copy(
        src_ref=src, dst_ref=dst, send_sem=send, recv_sem=recv, device_id=device, device_id_type=MESH
    )


def meet():
    x, me = lax.axis_index("heads"), lax.axis_index("ctx")
    barrier = pltpu.get_barrier_semaphore()
    for d in (1, 2, 3):
        pl.semaphore_signal(barrier, inc=1, device_id={"heads": lax.rem(x + d, 4)}, device_id_type=MESH)

    def greet(d, carry):
        pl.semaphore_signal(barrier, inc=1, device_id={"ctx": lax.rem(me + d, NBLK)}, device_id_type=MESH)
        return carry

    lax.fori_loop(1, NBLK, greet, 0)
    pl.semaphore_wait(barrier, NBLK - 1 + 3)


class Ring:
    def __init__(self, batch, half):
        x, y, z, core = place()
        self.half, self.core = half, core
        self.cols = pl.ds(batch * HALF + half * QUARTER, QUARTER)
        self.heads = range((2 * batch + half) * 2, (2 * batch + half + 1) * 2)
        self.a, self.b = (y, z) if half == 0 else (z, y)
        self.side = 1 - 2 * core

    def at_a(self, d):
        return lax.rem(self.a + d + 4, 4)

    def at_b(self, d):
        return lax.rem(self.b + d + 4, 4)

    def device(self, da, db):
        a, b = self.at_a(da), self.at_b(db)
        y, z = (a, b) if self.half == 0 else (b, a)
        return {"ctx": ctx_id(y, z, self.core)}

    def sibling(self):
        y, z = (self.a, self.b) if self.half == 0 else (self.b, self.a)
        return {"ctx": ctx_id(y, z, 1 - self.core)}

    def block(self, ref, a):
        y, z = (a, self.b) if self.half == 0 else (self.b, a)
        return ref.at[y, z, self.core, :, self.cols]

    def line(self, ref, b, core):
        return ref.at[:, b, core, :, self.cols] if self.half == 0 else ref.at[b, :, core, :, self.cols]

    def bare_line(self, ref, b):
        return ref.at[:, b, :, self.cols] if self.half == 0 else ref.at[b, :, :, self.cols]


def settle(send=None, recv=None):
    sem, ref = send or recv
    copy = remote(ref, ref, sem, sem, {"heads": lax.rem(lax.axis_index("heads") + 1, 4)})
    if send:
        copy.wait_send()
    else:
        copy.wait_recv()


class Mover:
    def __init__(self, batch, send, recv):
        self.send, self.recv = send, recv.at[batch]
        self.rings = [Ring(batch, 0), Ring(batch, 1)]

    def go(self, kind, n, src, dst, device):
        remote(src, dst, self.send.at[kind], self.recv.at[n], device).start()


def flush(send, windows):
    settle(send=(send.at[0], windows.at[pl.ds(0, 3), :, :, :, pl.ds(0, QUARTER)]))
    settle(send=(send.at[1], windows.at[pl.ds(0, 3)]))
    settle(send=(send.at[2], windows))


class Gather(Mover):
    def __init__(self, batch, out, send, recv):
        super().__init__(batch, send, recv)
        self.out = out

    def got(self, n, *index):
        settle(recv=(self.recv.at[n], self.out.at[(*index, slice(None), pl.ds(0, QUARTER))]))

    def a_send(self):
        for g in self.rings:
            own = g.block(self.out, g.a)
            for d in (1, 3, 2):
                self.go(0, 4, own, own, g.device(d, 0))

    def to_sibling(self, d):
        for g in self.rings:
            line = g.line(self.out, g.at_b(-d), g.core)
            self.go(2, d, line, line, g.sibling())

    def b_send(self):
        self.got(4, pl.ds(0, 3), 0, slice(None))
        for g in self.rings:
            own = g.line(self.out, g.b, g.core)
            for d in (1, 3):
                self.go(1, 5, own, own, g.device(0, d))
        self.to_sibling(0)

    def near(self):
        self.got(5, slice(None), slice(None), 0)
        for g in self.rings:
            line = g.line(self.out, g.at_b(-g.side), g.core)
            self.go(1, 6, line, line, g.device(0, g.side))
        self.to_sibling(1)
        self.to_sibling(3)

    def far(self):
        self.got(6, slice(None), 0, slice(None))
        self.to_sibling(2)

    def from_sibling(self, d):
        self.got(d, slice(None), 0, slice(None))


class Scatter(Mover):
    def __init__(self, batch, terms, sib, lines, blocks, send, recv):
        super().__init__(batch, send, recv)
        self.terms, self.sib, self.lines, self.blocks = terms, sib, lines.at[batch], blocks.at[batch]

    def to_sibling(self, h, d):
        g = self.rings[h]
        b = g.at_b(d)
        self.go(2, d, g.line(self.terms, b, 1 - g.core), g.bare_line(self.sib, b), g.sibling())

    def from_sibling(self, d):
        settle(recv=(self.recv.at[d], self.sib.at[pl.ds(0, 2), :, :, pl.ds(0, QUARTER)]))

    def b_send(self, d):
        self.from_sibling(d)
        for h, g in enumerate(self.rings):
            b = g.at_b(d)
            mine, other = g.line(self.terms, b, g.core), g.bare_line(self.sib, b)
            mine[...] = add(mine[...], other[...])
            self.go(1, 4, mine, self.lines.at[h, d - 1], g.device(0, d))

    def a_send(self):
        self.from_sibling(0)
        settle(recv=(self.recv.at[4], self.lines))
        for h, g in enumerate(self.rings):
            mine, other = g.line(self.terms, g.b, g.core), g.bare_line(self.sib, g.b)
            mine[...] = add(mine[...], other[...], *(self.lines[h, d] for d in range(3)))
            for d in (2, 1, 3):
                self.go(0, 5, g.block(self.terms, g.at_a(d)), self.blocks.at[h, d - 1], g.device(d, 0))

    def finish(self):
        settle(recv=(self.recv.at[5], self.blocks))
        for h, g in enumerate(self.rings):
            mine = g.block(self.terms, g.a)
            mine[...] = add(mine[...], *(self.blocks[h, d] for d in range(3)))


class Heads:
    def __init__(self, wide, own, inward, sems):
        x = lax.axis_index("heads")
        self.send, self.recv, local = (sems.at[n] for n in range(3))
        self.dst = own.at[pl.ds(0, 48), :] if inward else wide.at[:, pl.ds(0, 3 * WIDTH)]

        def cols(x):
            return wide.at[:, pl.ds(pl.multiple_of(x * WIDTH, WIDTH), WIDTH)]

        def rows(x):
            return own.at[pl.ds(pl.multiple_of(x * 16, 16), 16), :]

        for d in (1, 2, 3):
            to = lax.rem(x + d, 4)
            src, dst = (cols(to), rows(x)) if inward else (rows(to), cols(x))
            remote(src, dst, self.send, self.recv, {"heads": to}).start()
        src, dst = (cols(x), rows(x)) if inward else (rows(x), cols(x))
        self.local = pltpu.make_async_copy(src, dst, local)
        self.local.start()

    def arrived(self):
        self.local.wait()
        settle(recv=(self.recv, self.dst))

    def flush(self):
        settle(send=(self.send, self.dst))


def all_lanes(shape):
    return lax.broadcasted_iota(jnp.int32, shape, 1)


def fetch(ref, half, b, h):
    cols = pl.ds(h * DH, DH)
    tile = ref[:, b, :, :, cols] if half == 0 else ref[b, :, :, :, cols]
    return tile.reshape(LINE, DH)


def put(ref, half, b, h, tile):
    tile = tile.reshape(4, 2, ROWS, DH)
    cols = pl.ds(h * DH, DH)
    if half == 0:
        ref[:, b, :, :, cols] = tile
    else:
        ref[b, :, :, :, cols] = tile


def forward_line(ring, d, q, k, vx, weights, out, peaks, bias, first):
    half, b = ring.half, ring.at_b(-d)
    lane = all_lanes((LINE, DH))
    stats = jnp.zeros((LINE, DH), f32) if first else peaks[half, b]
    for h in ring.heads:
        scores = dot(fetch(q, half, b, h), k[:, h * DH : (h + 1) * DH], NT)
        if d == 0:
            late = scores[:, BLOCK - DH :] + bias[half]
            scores = jnp.concatenate([scores[:, : BLOCK - DH], late], axis=1)
        peak = jnp.max(scores, axis=1, keepdims=True)
        w = jnp.exp2((scores - peak) * SCALE2).astype(bf16)
        weights[h, b] = w
        both = dot(w, vx[h], NN)
        put(out, half, b, h, both[:, :DH].astype(bf16))
        stats = jnp.where(lane == h, peak * SCALE, stats)
        stats = jnp.where(lane == HEADS_DEV + h, both[:, DH:], stats)
    peaks[half, b] = stats


def scale_line(ring, d, factors, out):
    half, b = ring.half, ring.at_b(d)
    factor = (factors[:, b] if half == 0 else factors[b]).reshape(LINE, DH)
    for h in ring.heads:
        put(out, half, b, h, (fetch(out, half, b, h).astype(f32) * factor[:, h : h + 1]).astype(bf16))


def backward_line(ring, d, q, g, k, v, weights, factors, out, dq, dk, dv):
    half, b = ring.half, ring.at_b(d)
    factor = (factors[:, b] if half == 0 else factors[b]).reshape(LINE, DH)
    for h in ring.heads:
        cols = slice(h * DH, (h + 1) * DH)
        share, delta = factor[:, h : h + 1], factor[:, HEADS_DEV + h : HEADS_DEV + h + 1]
        grad = (fetch(g, half, b, h).astype(f32) * share).astype(bf16)
        if out is not None:
            put(out, half, b, h, (fetch(out, half, b, h).astype(f32) * share).astype(bf16))
        w = weights[h, b]
        dprob = dot(grad, v[:, cols], NT)
        dscores = (w.astype(f32) * (dprob - delta)).astype(bf16)
        dv[:, cols] += dot(w, grad, TN)
        dk[:, cols] += dot(dscores, fetch(q, half, b, h), TN)
        put(dq, half, b, h, (dot(dscores, k[:, cols], NN) * SCALE).astype(bf16))


def kernel(
    q_in, k_in, v_in, picks_in, g_in,
    out_ref, dq_ref, dk_ref, dv_ref,
    q, g, out, dq, k, v, picks, vx, weights, dk, dv, bias, live, peaks, own_peaks, factors, pick_head,
    tell, told, merged,
    sib, lines, blocks,
    gather_send, gather_recv, scatter_send, scatter_recv,
    heads_sems, stat_send, stat_recv, local,
):
    x, y, z, core = place()
    me = lax.axis_index("ctx")
    out_ref, dq_ref, dk_ref, dv_ref = out_ref.at[0], dq_ref.at[0], dk_ref.at[0], dv_ref.at[0]
    loads = [pltpu.make_async_copy(a, b, local.at[i]) for i, (a, b) in enumerate([(k_in, k), (v_in, v), (picks_in, picks)])]
    for load in loads:
        load.start()
    meet()
    in_q = Heads(q_in, q.at[y, z, core], True, heads_sems.at[0])
    in_g = Heads(g_in, g.at[y, z, core], True, heads_sems.at[1])
    move_q = [Gather(p, q, gather_send, gather_recv.at[0]) for p in (0, 1)]
    move_g = [Gather(p, g, gather_send, gather_recv.at[1]) for p in (0, 1)]
    sum_out, sum_dq = (
        [
            Scatter(p, terms, sib.at[n], lines.at[n], blocks.at[n], scatter_send, scatter_recv.at[n])
            for p in (0, 1)
        ]
        for n, terms in enumerate((out, dq))
    )
    rings = [move_q[p].rings for p in (0, 1)]
    lane = all_lanes((HEADS_DEV, DH))

    def forward(p, d):
        for ring in rings[p]:
            forward_line(ring, d, q, k, vx, weights, out, peaks, bias, p == 0)

    def tell_levels(p):
        active = lax.broadcasted_iota(jnp.int32, (HEADS_DEV, DH), 0) // 4 == p

        def tell_chip(i, carry):
            cy, cz = i // 4, lax.rem(i, 4)
            stats = peaks[0, cz, pl.ds(pl.multiple_of(cy * 2 * ROWS, 2 * ROWS), 2 * ROWS), :]
            stats = stats + peaks[1, cy, pl.ds(pl.multiple_of(cz * 2 * ROWS, 2 * ROWS), 2 * ROWS), :]
            cols = pl.ds(p * HALF, HALF)
            products = (g[cy, cz, :, :, cols].astype(f32) * out[cy, cz, :, :, cols].astype(f32)).reshape(2 * ROWS, HALF)
            high = products.astype(bf16)
            low = (products - high.astype(f32)).astype(bf16)
            turned = (stats + dot(high, pick_head[p], NN) + dot(low, pick_head[p], NN)).T
            total = jnp.where(active, turned[HEADS_DEV : 2 * HEADS_DEV], 1.0)
            peak = turned[:HEADS_DEV] + jnp.where(lane < ROWS, live[2 * i], live[2 * i + 1])
            own_peaks[p, i] = peak
            level = peak + jnp.log(total)
            delta = turned[2 * HEADS_DEV : 3 * HEADS_DEV] / total
            tell[p, 2 * i] = jnp.where(lane < ROWS, level, pltpu.roll(delta, ROWS, 1))
            tell[p, 2 * i + 1] = jnp.where(lane < ROWS, pltpu.roll(level, ROWS, 1), delta)
            return carry

        lax.fori_loop(0, NBLK // 2, tell_chip, 0, unroll=4)

        def send_level(d, carry):
            peer = lax.rem(me + d, NBLK)
            remote(tell.at[p, peer], told.at[p, me], stat_send.at[p, 0], stat_recv.at[p, 0], {"ctx": peer}).start()
            return carry

        lax.fori_loop(1, NBLK, send_level, 0)
        told[p, me] = tell[p, me]

    def hear(p, phase, ref):
        settle(recv=(stat_recv.at[p, phase], ref.at[p, pl.ds(0, NBLK - 1)]))

    def merge_levels(p):
        hear(p, 0, told)
        every = told[p]
        highest = jnp.max(every, axis=0)
        grown = jnp.exp(every - highest[None])
        total = jnp.sum(grown, axis=0)
        level = highest + jnp.log(total)
        delta = jnp.zeros((HEADS_DEV, DH), f32)
        for b in range(NBLK):
            delta = delta + pltpu.roll(grown[b], ROWS, 1) * every[b]
        delta = delta / pltpu.roll(total, ROWS, 1)
        merged[p, me] = jnp.where(lane < ROWS, level, delta)
        mine = merged.at[p, me]

        def share_level(d, carry):
            peer = lax.rem(me + d, NBLK)
            remote(mine, mine, stat_send.at[p, 1], stat_recv.at[p, 1], {"ctx": peer}).start()
            return carry

        lax.fori_loop(1, NBLK, share_level, 0)

    def weigh(p):
        hear(p, 1, merged)

        def weigh_chip(i, carry):
            first, second = merged[p, 2 * i], merged[p, 2 * i + 1]
            level = jnp.where(lane < ROWS, first, pltpu.roll(second, ROWS, 1))
            delta = jnp.where(lane < ROWS, pltpu.roll(first, ROWS, 1), second)
            share = jnp.exp(own_peaks[p, i] - level)
            rows = jnp.concatenate([share, share * delta], axis=0)
            factors[p, i // 4, lax.rem(i, 4), :, : 2 * HEADS_DEV] = rows.T
            return carry

        lax.fori_loop(0, NBLK // 2, weigh_chip, 0, unroll=4)

    def backward(p, d, scale=True, between=None):
        for half, ring in enumerate(rings[p]):
            backward_line(ring, d, q, g, k, v, weights, factors.at[p], out if scale else None, dq, dk, dv)
            if scale:
                sum_out[p].to_sibling(half, d)
            sum_dq[p].to_sibling(half, d)
            if half == 0 and between:
                between()

    def scale(p, d):
        for half, ring in enumerate(rings[p]):
            scale_line(ring, d, factors.at[p], out)
            sum_out[p].to_sibling(half, d)

    def b_send(p, d):
        sum_out[p].b_send(d)
        sum_dq[p].b_send(d)

    saves = []

    def save(p):
        for h in range(4 * p, 4 * p + 4):
            cols = slice(h * DH, (h + 1) * DH)
            k[:, cols] = (dk[:, cols] * SCALE).astype(bf16)
            v[:, cols] = dv[:, cols].astype(bf16)
        cols = pl.ds(p * HALF, HALF)
        for n, (src, dst) in enumerate([(k, dk_ref), (v, dv_ref)]):
            saves.append(pltpu.make_async_copy(src.at[:, cols], dst.at[:, cols], local.at[2 * p + n]))
            saves[-1].start()

    for load in loads:
        load.wait()
    for h in range(HEADS_DEV):
        vx[h, :, :DH] = v[:, h * DH : (h + 1) * DH]
        vx[h, :, DH:] = jnp.ones((BLOCK, DH), bf16)
    in_q.arrived()
    move_q[0].a_send()
    in_g.arrived()
    move_g[0].a_send()
    move_q[0].b_send()
    move_g[0].b_send()
    move_q[1].a_send()
    move_g[1].a_send()
    bias[...] = jnp.zeros_like(bias)
    row = lax.broadcasted_iota(jnp.int32, (ROWS, DH), 0)
    late = jnp.where(all_lanes((ROWS, DH)) - (DH - ROWS) > row, -BIG, 0.0)
    for half, r in enumerate(rings[0]):
        bias[half, pl.ds(pl.multiple_of((r.a * 2 + core) * ROWS, ROWS), ROWS), :] = late
    col = lax.broadcasted_iota(jnp.int32, (HALF, DH), 0) // DH
    for p in (0, 1):
        pick_head[p] = jnp.where(all_lanes((HALF, DH)) == col + 2 * HEADS_DEV + 4 * p, 1.0, 0.0).astype(bf16)
    dk[...] = jnp.zeros_like(dk)
    dv[...] = jnp.zeros_like(dv)
    chosen = jnp.max(jnp.where(picks[...] == me, 0.0, -BIG), axis=0, keepdims=True)
    for b in range(NBLK):
        live[b] = jnp.broadcast_to(chosen[:, b : b + 1], (HEADS_DEV, DH))

    move_q[0].from_sibling(0)
    forward(0, 0)
    move_q[0].near()
    move_g[0].near()
    move_q[1].b_send()
    move_q[0].from_sibling(1)
    forward(0, 1)
    move_g[1].b_send()
    move_q[0].from_sibling(3)
    forward(0, 3)
    move_q[0].far()
    move_g[0].far()
    move_q[1].from_sibling(0)
    forward(1, 0)
    move_q[0].from_sibling(2)
    forward(0, 2)
    move_q[1].near()
    move_g[1].near()
    for d in (0, 1, 3, 2):
        move_g[0].from_sibling(d)
    tell_levels(0)
    move_q[1].from_sibling(1)
    forward(1, 1)
    move_q[1].far()
    move_g[1].far()
    move_q[1].from_sibling(3)
    forward(1, 3)
    merge_levels(0)
    move_q[1].from_sibling(2)
    forward(1, 2)
    for d in (0, 1, 3, 2):
        move_g[1].from_sibling(d)
    tell_levels(1)
    weigh(0)

    backward(0, 2)
    merge_levels(1)
    backward(0, 1, between=lambda: b_send(0, 2))
    backward(0, 3, between=lambda: b_send(0, 1))
    weigh(1)
    for p, d in ((0, 0), (1, 3), (1, 0)):
        scale(p, d)
    backward(1, 2, between=lambda: b_send(0, 3))
    sum_out[1].b_send(3)
    backward(1, 1, between=lambda: b_send(1, 2))
    sum_out[0].a_send()
    backward(1, 3, scale=False, between=lambda: b_send(1, 1))
    backward(0, 0, scale=False, between=lambda: sum_dq[1].b_send(3))
    sum_out[0].finish()
    sum_out[1].a_send()
    backward(1, 0, scale=False, between=sum_dq[0].a_send)
    save(0)
    sum_dq[1].a_send()
    sum_out[1].finish()
    out_heads = Heads(out_ref, out.at[y, z, core], False, heads_sems.at[2])
    save(1)
    sum_dq[0].finish()
    sum_dq[1].finish()
    dq_heads = Heads(dq_ref, dq.at[y, z, core], False, heads_sems.at[3])
    out_heads.arrived()
    for p in (0, 1):
        for phase in (0, 1):
            settle(send=(stat_send.at[p, phase], tell.at[p, pl.ds(0, NBLK - 1)]))
    flush(gather_send, q)
    flush(scatter_send, q)
    for heads in (in_q, in_g, out_heads):
        heads.flush()
    for copy in saves:
        copy.wait()
    dq_heads.arrived()
    dq_heads.flush()


def hand_out(*refs):
    copies = [pltpu.make_async_copy(refs[i], refs[4 + i], refs[8].at[i]) for i in range(4)]
    for copy in copies:
        copy.start()
    for copy in copies:
        copy.wait()


def body(queries, keys, values, picks, d_out):
    rows, wide = jax.ShapeDtypeStruct((1, 16, 4 * WIDTH), bf16), jax.ShapeDtypeStruct((1, BLOCK, WIDTH), bf16)
    anywhere = pl.BlockSpec(memory_space=pl.ANY)
    windows = pltpu.VMEM((4, 4, 2, ROWS, WIDTH), bf16)
    levels = pltpu.VMEM((2, NBLK, HEADS_DEV, DH), f32)
    dma = pltpu.SemaphoreType.DMA
    out, dq, dk, dv = pl.pallas_call(
        kernel,
        out_shape=(rows, rows, wide, wide),
        in_specs=[anywhere] * 5,
        out_specs=[anywhere] * 4,
        scratch_shapes=[
            windows, windows, windows, windows,
            pltpu.VMEM((BLOCK, WIDTH), bf16), pltpu.VMEM((BLOCK, WIDTH), bf16),
            pltpu.VMEM(picks.shape[::-1], jnp.int32),
            pltpu.VMEM((HEADS_DEV, BLOCK, 2 * DH), bf16),
            pltpu.VMEM((HEADS_DEV, 4, LINE, BLOCK), bf16),
            pltpu.VMEM((BLOCK, WIDTH), f32), pltpu.VMEM((BLOCK, WIDTH), f32),
            pltpu.VMEM((2, LINE, DH), f32),
            pltpu.VMEM((NBLK, HEADS_DEV, DH), f32),
            pltpu.VMEM((2, 4, LINE, DH), f32),
            pltpu.VMEM((2, NBLK // 2, HEADS_DEV, DH), f32), pltpu.VMEM((2, 4, 4, 2 * ROWS, DH), f32),
            pltpu.VMEM((2, HALF, DH), bf16),
            levels, levels, levels,
            pltpu.VMEM((2, 4, 4, ROWS, WIDTH), bf16),
            pltpu.VMEM((2, 2, 2, 3, 4, ROWS, QUARTER), bf16), pltpu.VMEM((2, 2, 2, 3, ROWS, QUARTER), bf16),
            dma((3,)), dma((2, 2, 7)), dma((3,)), dma((2, 2, 6)),
            dma((4, 3)), dma((2, 2)), dma((2, 2)), dma((4,)),
        ],
        compiler_params=pltpu.CompilerParams(collective_id=0, has_side_effects=True, vmem_limit_bytes=63 << 20),
        name="block_attention",
    )(queries[0], keys[0], values[0], picks.T, d_out[0])
    return pl.pallas_call(
        hand_out,
        out_shape=(out, dq, dk, dv),
        in_specs=[pl.BlockSpec(memory_space=pltpu.VMEM)] * 4,
        out_specs=[anywhere] * 4,
        scratch_shapes=[dma((4,))],
        name="hand_out",
    )(out, dq, dk, dv)


def solution(mesh):
    rows, blocks = P("ctx", "heads", None), P("ctx", None, "heads")
    return jax.shard_map(
        body,
        mesh=mesh,
        in_specs=(rows, blocks, blocks, P(), rows),
        out_specs=(rows, rows, blocks, blocks),
        check_vma=False,
    )
```

```python
import functools
import math

import jax
import jax.numpy as jnp
from jax import lax
from jax.experimental import pallas as pl
from jax.experimental.pallas import tpu as pltpu
from jax.sharding import PartitionSpec as P

MESH = pl.DeviceIdType.MESH
DH = 128
HEADS_DEV = 8
BLOCK = 512
NBLK = 32
ROWS = 64
WIDTH = HEADS_DEV * DH
HALF = WIDTH // 2
QUARTER = WIDTH // 4
LINE = 8 * ROWS
SCALE = 1.0 / math.sqrt(DH)
SCALE2 = SCALE * math.log2(math.e)
BIG = 1e30
f32 = jnp.float32
bf16 = jnp.bfloat16

NT = (((1,), (1,)), ((), ()))
NN = (((1,), (0,)), ((), ()))
TN = (((0,), (0,)), ((), ()))


def dot(a, b, dims):
    return lax.dot_general(a, b, dims, preferred_element_type=f32)


def add(*parts):
    total = parts[0].astype(f32)
    for part in parts[1:]:
        total = total + part.astype(f32)
    return total.astype(bf16)


def place():
    x = lax.axis_index("heads")
    ctx = lax.axis_index("ctx")
    return x, ctx // 8, lax.rem(ctx // 2, 4), lax.rem(ctx, 2)


def ctx_id(y, z, core):
    return (y * 4 + z) * 2 + core


def remote(src, dst, send, recv, device):
    return pltpu.make_async_remote_copy(
        src_ref=src, dst_ref=dst, send_sem=send, recv_sem=recv, device_id=device, device_id_type=MESH
    )


def meet():
    x, me = lax.axis_index("heads"), lax.axis_index("ctx")
    barrier = pltpu.get_barrier_semaphore()
    for d in (1, 2, 3):
        pl.semaphore_signal(barrier, inc=1, device_id={"heads": lax.rem(x + d, 4)}, device_id_type=MESH)

    def greet(d, carry):
        pl.semaphore_signal(barrier, inc=1, device_id={"ctx": lax.rem(me + d, NBLK)}, device_id_type=MESH)
        return carry

    lax.fori_loop(1, NBLK, greet, 0)
    pl.semaphore_wait(barrier, NBLK - 1 + 3)


class Ring:
    def __init__(self, batch, half):
        x, y, z, core = place()
        self.half, self.core = half, core
        self.cols = pl.ds(batch * HALF + half * QUARTER, QUARTER)
        self.heads = range((2 * batch + half) * 2, (2 * batch + half + 1) * 2)
        self.a, self.b = (y, z) if half == 0 else (z, y)
        self.side = 1 - 2 * core

    def at_a(self, d):
        return lax.rem(self.a + d + 4, 4)

    def at_b(self, d):
        return lax.rem(self.b + d + 4, 4)

    def device(self, da, db):
        a, b = self.at_a(da), self.at_b(db)
        y, z = (a, b) if self.half == 0 else (b, a)
        return {"ctx": ctx_id(y, z, self.core)}

    def sibling(self):
        y, z = (self.a, self.b) if self.half == 0 else (self.b, self.a)
        return {"ctx": ctx_id(y, z, 1 - self.core)}

    def block(self, ref, a):
        y, z = (a, self.b) if self.half == 0 else (self.b, a)
        return ref.at[y, z, self.core, :, self.cols]

    def line(self, ref, b, core):
        return ref.at[:, b, core, :, self.cols] if self.half == 0 else ref.at[b, :, core, :, self.cols]

    def bare_line(self, ref, b):
        return ref.at[:, b, :, self.cols] if self.half == 0 else ref.at[b, :, :, self.cols]


def settle(send=None, recv=None):
    sem, ref = send or recv
    copy = remote(ref, ref, sem, sem, {"heads": lax.rem(lax.axis_index("heads") + 1, 4)})
    if send:
        copy.wait_send()
    else:
        copy.wait_recv()


class Mover:
    def __init__(self, batch, send, recv):
        self.send, self.recv = send, recv.at[batch]
        self.rings = [Ring(batch, 0), Ring(batch, 1)]

    def go(self, kind, n, src, dst, device):
        remote(src, dst, self.send.at[kind], self.recv.at[n], device).start()


def flush(send, windows):
    settle(send=(send.at[0], windows.at[pl.ds(0, 3), :, :, :, pl.ds(0, QUARTER)]))
    settle(send=(send.at[1], windows.at[pl.ds(0, 3)]))
    settle(send=(send.at[2], windows))


class Gather(Mover):
    def __init__(self, batch, out, send, recv):
        super().__init__(batch, send, recv)
        self.out = out

    def got(self, n, *index):
        settle(recv=(self.recv.at[n], self.out.at[(*index, slice(None), pl.ds(0, QUARTER))]))

    def a_send(self):
        for g in self.rings:
            own = g.block(self.out, g.a)
            for d in (1, 3, 2):
                self.go(0, 4, own, own, g.device(d, 0))

    def to_sibling(self, d):
        for g in self.rings:
            line = g.line(self.out, g.at_b(-d), g.core)
            self.go(2, d, line, line, g.sibling())

    def b_send(self):
        self.got(4, pl.ds(0, 3), 0, slice(None))
        for g in self.rings:
            own = g.line(self.out, g.b, g.core)
            for d in (1, 3):
                self.go(1, 5, own, own, g.device(0, d))
        self.to_sibling(0)

    def near(self):
        self.got(5, slice(None), slice(None), 0)
        for g in self.rings:
            line = g.line(self.out, g.at_b(-g.side), g.core)
            self.go(1, 6, line, line, g.device(0, g.side))
        self.to_sibling(1)
        self.to_sibling(3)

    def far(self):
        self.got(6, slice(None), 0, slice(None))
        self.to_sibling(2)

    def from_sibling(self, d):
        self.got(d, slice(None), 0, slice(None))


class Scatter(Mover):
    def __init__(self, batch, terms, sib, lines, blocks, send, recv):
        super().__init__(batch, send, recv)
        self.terms, self.sib, self.lines, self.blocks = terms, sib, lines.at[batch], blocks.at[batch]

    def to_sibling(self, h, d):
        g = self.rings[h]
        b = g.at_b(d)
        self.go(2, d, g.line(self.terms, b, 1 - g.core), g.bare_line(self.sib, b), g.sibling())

    def from_sibling(self, d):
        settle(recv=(self.recv.at[d], self.sib.at[pl.ds(0, 2), :, :, pl.ds(0, QUARTER)]))

    def b_send(self, d):
        self.from_sibling(d)
        for h, g in enumerate(self.rings):
            b = g.at_b(d)
            mine, other = g.line(self.terms, b, g.core), g.bare_line(self.sib, b)
            mine[...] = mine[...] + other[...]
            self.go(1, 4, mine, self.lines.at[h, d - 1], g.device(0, d))

    def a_send(self):
        self.from_sibling(0)
        settle(recv=(self.recv.at[4], self.lines))
        for h, g in enumerate(self.rings):
            mine, other = g.line(self.terms, g.b, g.core), g.bare_line(self.sib, g.b)
            mine[...] = add(mine[...], other[...], *(self.lines[h, d] for d in range(3)))
            for d in (2, 1, 3):
                self.go(0, 5, g.block(self.terms, g.at_a(d)), self.blocks.at[h, d - 1], g.device(d, 0))

    def finish(self):
        settle(recv=(self.recv.at[5], self.blocks))
        for h, g in enumerate(self.rings):
            mine = g.block(self.terms, g.a)
            mine[...] = add(mine[...], *(self.blocks[h, d] for d in range(3)))


class Heads:
    def __init__(self, wide, own, inward, sems):
        x = lax.axis_index("heads")
        self.send, self.recv, local = (sems.at[n] for n in range(3))
        self.dst = own.at[pl.ds(0, 48), :] if inward else wide.at[:, pl.ds(0, 3 * WIDTH)]

        def cols(x):
            return wide.at[:, pl.ds(pl.multiple_of(x * WIDTH, WIDTH), WIDTH)]

        def rows(x):
            return own.at[pl.ds(pl.multiple_of(x * 16, 16), 16), :]

        for d in (1, 2, 3):
            to = lax.rem(x + d, 4)
            src, dst = (cols(to), rows(x)) if inward else (rows(to), cols(x))
            remote(src, dst, self.send, self.recv, {"heads": to}).start()
        src, dst = (cols(x), rows(x)) if inward else (rows(x), cols(x))
        self.local = pltpu.make_async_copy(src, dst, local)
        self.local.start()

    def arrived(self):
        self.local.wait()
        settle(recv=(self.recv, self.dst))

    def flush(self):
        settle(send=(self.send, self.dst))


def all_lanes(shape):
    return lax.broadcasted_iota(jnp.int32, shape, 1)


def fetch(ref, half, b, h):
    cols = pl.ds(h * DH, DH)
    tile = ref[:, b, :, :, cols] if half == 0 else ref[b, :, :, :, cols]
    return tile.reshape(LINE, DH)


def put(ref, half, b, h, tile):
    tile = tile.reshape(4, 2, ROWS, DH)
    cols = pl.ds(h * DH, DH)
    if half == 0:
        ref[:, b, :, :, cols] = tile
    else:
        ref[b, :, :, :, cols] = tile


def forward_line(ring, d, q, k, vx, weights, out, peaks, bias, first):
    half, b = ring.half, ring.at_b(-d)
    lane = all_lanes((LINE, DH))
    stats = jnp.zeros((LINE, DH), f32) if first else peaks[half, b]
    for h in ring.heads:
        scores = dot(fetch(q, half, b, h), k[:, h * DH : (h + 1) * DH], NT)
        if d == 0:
            late = scores[:, BLOCK - DH :] + bias[half]
            scores = jnp.concatenate([scores[:, : BLOCK - DH], late], axis=1)
        peak = jnp.max(scores, axis=1, keepdims=True)
        w = jnp.exp2((scores - peak) * SCALE2).astype(bf16)
        weights[h, b] = w
        both = dot(w, vx[h], NN)
        put(out, half, b, h, both[:, :DH].astype(bf16))
        stats = jnp.where(lane == h, peak * SCALE, stats)
        stats = jnp.where(lane == HEADS_DEV + h, both[:, DH:], stats)
    peaks[half, b] = stats


def scale_line(ring, d, factors, out):
    half, b = ring.half, ring.at_b(d)
    factor = (factors[:, b] if half == 0 else factors[b]).reshape(LINE, DH)
    for h in ring.heads:
        put(out, half, b, h, (fetch(out, half, b, h).astype(f32) * factor[:, h : h + 1]).astype(bf16))


def backward_line(ring, d, q, g, k, v, weights, factors, out, dq, dk, dv):
    half, b = ring.half, ring.at_b(d)
    factor = (factors[:, b] if half == 0 else factors[b]).reshape(LINE, DH)
    for h in ring.heads:
        cols = slice(h * DH, (h + 1) * DH)
        share, delta = factor[:, h : h + 1], factor[:, HEADS_DEV + h : HEADS_DEV + h + 1]
        grad = (fetch(g, half, b, h).astype(f32) * share).astype(bf16)
        if out is not None:
            put(out, half, b, h, (fetch(out, half, b, h).astype(f32) * share).astype(bf16))
        w = weights[h, b]
        dprob = dot(grad, v[:, cols], NT)
        dscores = (w.astype(f32) * (dprob - delta)).astype(bf16)
        dv[h] += dot(grad, w, TN)
        dk[h] += dot(fetch(q, half, b, h), dscores, TN)
        put(dq, half, b, h, (dot(dscores, k[:, cols], NN) * SCALE).astype(bf16))


def kernel(
    q_in, k_in, v_in, picks_in, g_in,
    out_ref, dq_ref, dk_ref, dv_ref,
    q, g, out, dq, k, v, picks, vx, weights, dk, dv, bias, live, peaks, own_peaks, factors, pick_head,
    tell, told, merged,
    sib, lines, blocks,
    gather_send, gather_recv, scatter_send, scatter_recv,
    heads_sems, stat_send, stat_recv, local,
):
    x, y, z, core = place()
    me = lax.axis_index("ctx")
    out_ref, dq_ref, dk_ref, dv_ref = out_ref.at[0], dq_ref.at[0], dk_ref.at[0], dv_ref.at[0]
    loads = [pltpu.make_async_copy(a, b, local.at[i]) for i, (a, b) in enumerate([(k_in, k), (v_in, v), (picks_in, picks)])]
    for load in loads:
        load.start()
    meet()
    in_q = Heads(q_in, q.at[y, z, core], True, heads_sems.at[0])
    in_g = Heads(g_in, g.at[y, z, core], True, heads_sems.at[1])
    move_q = [Gather(p, q, gather_send, gather_recv.at[0]) for p in (0, 1)]
    move_g = [Gather(p, g, gather_send, gather_recv.at[1]) for p in (0, 1)]
    sum_out, sum_dq = (
        [
            Scatter(p, terms, sib.at[n], lines.at[n], blocks.at[n], scatter_send, scatter_recv.at[n])
            for p in (0, 1)
        ]
        for n, terms in enumerate((out, dq))
    )
    rings = [move_q[p].rings for p in (0, 1)]
    lane = all_lanes((HEADS_DEV, DH))

    def forward(p, d):
        for ring in rings[p]:
            forward_line(ring, d, q, k, vx, weights, out, peaks, bias, p == 0)

    def tell_levels(p):
        active = lax.broadcasted_iota(jnp.int32, (HEADS_DEV, DH), 0) // 4 == p

        def tell_chip(i, carry):
            cy, cz = i // 4, lax.rem(i, 4)
            stats = peaks[0, cz, pl.ds(pl.multiple_of(cy * 2 * ROWS, 2 * ROWS), 2 * ROWS), :]
            stats = stats + peaks[1, cy, pl.ds(pl.multiple_of(cz * 2 * ROWS, 2 * ROWS), 2 * ROWS), :]
            cols = pl.ds(p * HALF, HALF)
            products = (g[cy, cz, :, :, cols].astype(f32) * out[cy, cz, :, :, cols].astype(f32)).reshape(2 * ROWS, HALF)
            high = products.astype(bf16)
            low = (products - high.astype(f32)).astype(bf16)
            turned = (stats + dot(high, pick_head[p], NN) + dot(low, pick_head[p], NN)).T
            total = jnp.where(active, turned[HEADS_DEV : 2 * HEADS_DEV], 1.0)
            peak = turned[:HEADS_DEV] + jnp.where(lane < ROWS, live[2 * i], live[2 * i + 1])
            own_peaks[p, i] = peak
            level = peak + jnp.log(total)
            delta = turned[2 * HEADS_DEV : 3 * HEADS_DEV] / total
            tell[p, 2 * i] = jnp.where(lane < ROWS, level, pltpu.roll(delta, ROWS, 1))
            tell[p, 2 * i + 1] = jnp.where(lane < ROWS, pltpu.roll(level, ROWS, 1), delta)
            return carry

        lax.fori_loop(0, NBLK // 2, tell_chip, 0, unroll=4)

        def send_level(d, carry):
            peer = lax.rem(me + d, NBLK)
            remote(tell.at[p, peer], told.at[p, me], stat_send.at[p, 0], stat_recv.at[p, 0], {"ctx": peer}).start()
            return carry

        lax.fori_loop(1, NBLK, send_level, 0)
        told[p, me] = tell[p, me]

    def hear(p, phase, ref):
        settle(recv=(stat_recv.at[p, phase], ref.at[p, pl.ds(0, NBLK - 1)]))

    def merge_levels(p):
        hear(p, 0, told)
        every = told[p]
        highest = jnp.max(every, axis=0)
        grown = jnp.exp(every - highest[None])
        total = jnp.sum(grown, axis=0)
        level = highest + jnp.log(total)
        delta = jnp.zeros((HEADS_DEV, DH), f32)
        for b in range(NBLK):
            delta = delta + pltpu.roll(grown[b], ROWS, 1) * every[b]
        delta = delta / pltpu.roll(total, ROWS, 1)
        merged[p, me] = jnp.where(lane < ROWS, level, delta)
        mine = merged.at[p, me]

        def share_level(d, carry):
            peer = lax.rem(me + d, NBLK)
            remote(mine, mine, stat_send.at[p, 1], stat_recv.at[p, 1], {"ctx": peer}).start()
            return carry

        lax.fori_loop(1, NBLK, share_level, 0)

    def weigh(p):
        hear(p, 1, merged)

        def weigh_chip(i, carry):
            first, second = merged[p, 2 * i], merged[p, 2 * i + 1]
            level = jnp.where(lane < ROWS, first, pltpu.roll(second, ROWS, 1))
            delta = jnp.where(lane < ROWS, pltpu.roll(first, ROWS, 1), second)
            share = jnp.exp(own_peaks[p, i] - level)
            rows = jnp.concatenate([share, share * delta], axis=0)
            factors[p, i // 4, lax.rem(i, 4), :, : 2 * HEADS_DEV] = rows.T
            return carry

        lax.fori_loop(0, NBLK // 2, weigh_chip, 0, unroll=4)

    def backward(p, d, scale=True, between=None):
        for half, ring in enumerate(rings[p]):
            backward_line(ring, d, q, g, k, v, weights, factors.at[p], out if scale else None, dq, dk, dv)
            if scale:
                sum_out[p].to_sibling(half, d)
            sum_dq[p].to_sibling(half, d)
            if half == 0 and between:
                between()

    def scale(p, d):
        for half, ring in enumerate(rings[p]):
            scale_line(ring, d, factors.at[p], out)
            sum_out[p].to_sibling(half, d)

    def b_send(p, d):
        sum_out[p].b_send(d)
        sum_dq[p].b_send(d)

    saves = []

    def save(p):
        for h in range(4 * p, 4 * p + 4):
            cols = slice(h * DH, (h + 1) * DH)
            k[:, cols] = (dk[h] * SCALE).T.astype(bf16)
            v[:, cols] = dv[h].T.astype(bf16)
        cols = pl.ds(p * HALF, HALF)
        for n, (src, dst) in enumerate([(k, dk_ref), (v, dv_ref)]):
            saves.append(pltpu.make_async_copy(src.at[:, cols], dst.at[:, cols], local.at[2 * p + n]))
            saves[-1].start()

    for load in loads:
        load.wait()
    for h in range(HEADS_DEV):
        vx[h, :, :DH] = v[:, h * DH : (h + 1) * DH]
        vx[h, :, DH:] = jnp.ones((BLOCK, DH), bf16)
    in_q.arrived()
    move_q[0].a_send()
    in_g.arrived()
    move_g[0].a_send()
    move_q[0].b_send()
    move_q[1].a_send()
    bias[...] = jnp.zeros_like(bias)
    row = lax.broadcasted_iota(jnp.int32, (ROWS, DH), 0)
    late = jnp.where(all_lanes((ROWS, DH)) - (DH - ROWS) > row, -BIG, 0.0)
    for half, r in enumerate(rings[0]):
        bias[half, pl.ds(pl.multiple_of((r.a * 2 + core) * ROWS, ROWS), ROWS), :] = late
    col = lax.broadcasted_iota(jnp.int32, (HALF, DH), 0) // DH
    for p in (0, 1):
        pick_head[p] = jnp.where(all_lanes((HALF, DH)) == col + 2 * HEADS_DEV + 4 * p, 1.0, 0.0).astype(bf16)
    dk[...] = jnp.zeros_like(dk)
    dv[...] = jnp.zeros_like(dv)
    chosen = jnp.max(jnp.where(picks[...] == me, 0.0, -BIG), axis=0, keepdims=True)
    for b in range(NBLK):
        live[b] = jnp.broadcast_to(chosen[:, b : b + 1], (HEADS_DEV, DH))

    move_g[0].b_send()
    move_g[1].a_send()
    move_q[0].from_sibling(0)
    forward(0, 0)
    move_q[0].near()
    move_g[0].near()
    move_q[1].b_send()
    move_q[0].from_sibling(1)
    forward(0, 1)
    move_g[1].b_send()
    move_q[0].from_sibling(3)
    forward(0, 3)
    move_q[0].far()
    move_g[0].far()
    move_q[1].from_sibling(0)
    forward(1, 0)
    move_q[0].from_sibling(2)
    forward(0, 2)
    move_q[1].near()
    for d in (0, 1, 3, 2):
        move_g[0].from_sibling(d)
    tell_levels(0)
    move_g[1].near()
    move_q[1].from_sibling(1)
    forward(1, 1)
    move_q[1].far()
    move_g[1].far()
    move_q[1].from_sibling(3)
    forward(1, 3)
    merge_levels(0)
    move_q[1].from_sibling(2)
    forward(1, 2)
    for d in (0, 1, 3, 2):
        move_g[1].from_sibling(d)
    tell_levels(1)
    weigh(0)

    backward(0, 2)
    merge_levels(1)
    backward(0, 1, between=lambda: b_send(0, 2))
    backward(0, 3, between=lambda: b_send(0, 1))
    weigh(1)
    scale(1, 3)
    scale(1, 1)
    backward(1, 2, between=lambda: b_send(0, 3))
    sum_out[1].b_send(3)
    sum_out[1].b_send(1)
    backward(1, 1, scale=False, between=lambda: b_send(1, 2))
    backward(1, 3, scale=False, between=lambda: sum_dq[1].b_send(1))
    scale(0, 0)
    scale(1, 0)
    sum_dq[1].b_send(3)
    backward(0, 0, scale=False, between=sum_out[0].a_send)
    sum_dq[0].a_send()
    backward(1, 0, scale=False, between=sum_out[1].a_send)
    save(0)
    sum_dq[1].a_send()
    sum_out[0].finish()
    sum_out[1].finish()
    out_heads = Heads(out_ref, out.at[y, z, core], False, heads_sems.at[2])
    sum_dq[0].finish()
    save(1)
    sum_dq[1].finish()
    dq_heads = Heads(dq_ref, dq.at[y, z, core], False, heads_sems.at[3])
    out_heads.arrived()
    for p in (0, 1):
        for phase in (0, 1):
            settle(send=(stat_send.at[p, phase], tell.at[p, pl.ds(0, NBLK - 1)]))
    flush(gather_send, q)
    flush(scatter_send, q)
    for heads in (in_q, in_g, out_heads):
        heads.flush()
    for copy in saves:
        copy.wait()
    dq_heads.arrived()
    dq_heads.flush()


def hand_out(*refs):
    given, taken, held, (arrive, leave) = refs[:4], refs[4:8], refs[8:12], refs[12:]
    loads = [pltpu.make_async_copy(given[i], held[i], arrive.at[i]) for i in range(4)]
    stores = [pltpu.make_async_copy(held[i], taken[i], leave.at[i]) for i in range(4)]
    for i in (2, 3, 0, 1):
        loads[i].start()
    for i in (2, 3, 0, 1):
        loads[i].wait()
        stores[i].start()
    for store in stores:
        store.wait()


def body(queries, keys, values, picks, d_out):
    rows, wide = jax.ShapeDtypeStruct((1, 16, 4 * WIDTH), bf16), jax.ShapeDtypeStruct((1, BLOCK, WIDTH), bf16)
    anywhere = pl.BlockSpec(memory_space=pl.ANY)
    windows = pltpu.VMEM((4, 4, 2, ROWS, WIDTH), bf16)
    levels = pltpu.VMEM((2, NBLK, HEADS_DEV, DH), f32)
    dma = pltpu.SemaphoreType.DMA
    out, dq, dk, dv = pl.pallas_call(
        kernel,
        out_shape=(rows, rows, wide, wide),
        in_specs=[anywhere] * 5,
        out_specs=[anywhere] * 4,
        scratch_shapes=[
            windows, windows, windows, windows,
            pltpu.VMEM((BLOCK, WIDTH), bf16), pltpu.VMEM((BLOCK, WIDTH), bf16),
            pltpu.VMEM(picks.shape[::-1], jnp.int32),
            pltpu.VMEM((HEADS_DEV, BLOCK, 2 * DH), bf16),
            pltpu.VMEM((HEADS_DEV, 4, LINE, BLOCK), bf16),
            pltpu.VMEM((HEADS_DEV, DH, BLOCK), f32), pltpu.VMEM((HEADS_DEV, DH, BLOCK), f32),
            pltpu.VMEM((2, LINE, DH), f32),
            pltpu.VMEM((NBLK, HEADS_DEV, DH), f32),
            pltpu.VMEM((2, 4, LINE, DH), f32),
            pltpu.VMEM((2, NBLK // 2, HEADS_DEV, DH), f32), pltpu.VMEM((2, 4, 4, 2 * ROWS, DH), f32),
            pltpu.VMEM((2, HALF, DH), bf16),
            levels, levels, levels,
            pltpu.VMEM((2, 4, 4, ROWS, WIDTH), bf16),
            pltpu.VMEM((2, 2, 2, 3, 4, ROWS, QUARTER), bf16), pltpu.VMEM((2, 2, 2, 3, ROWS, QUARTER), bf16),
            dma((3,)), dma((2, 2, 7)), dma((3,)), dma((2, 2, 6)),
            dma((4, 3)), dma((2, 2)), dma((2, 2)), dma((4,)),
        ],
        compiler_params=pltpu.CompilerParams(collective_id=0, has_side_effects=True, vmem_limit_bytes=63 << 20),
        name="block_attention",
    )(queries[0], keys[0], values[0], picks.T, d_out[0])
    return pl.pallas_call(
        hand_out,
        out_shape=(out, dq, dk, dv),
        in_specs=[anywhere] * 4,
        out_specs=[anywhere] * 4,
        scratch_shapes=[pltpu.VMEM(a.shape, bf16) for a in (out, dq, dk, dv)] + [dma((4,)), dma((4,))],
        compiler_params=pltpu.CompilerParams(vmem_limit_bytes=63 << 20),
        name="hand_out",
    )(out, dq, dk, dv)


def solution(mesh):
    rows, blocks = P("ctx", "heads", None), P("ctx", None, "heads")
    return jax.shard_map(
        body,
        mesh=mesh,
        in_specs=(rows, blocks, blocks, P(), rows),
        out_specs=(rows, rows, blocks, blocks),
        check_vma=False,
    )
```

```python
import functools
import math

import jax
import jax.numpy as jnp
from jax import lax
from jax.experimental import pallas as pl
from jax.experimental.pallas import tpu as pltpu
from jax.sharding import PartitionSpec as P

MESH = pl.DeviceIdType.MESH
DH = 128
HEADS_DEV = 8
BLOCK = 512
NBLK = 32
ROWS = 64
WIDTH = HEADS_DEV * DH
HALF = WIDTH // 2
QUARTER = WIDTH // 4
LINE = 8 * ROWS
SCALE = 1.0 / math.sqrt(DH)
SCALE2 = SCALE * math.log2(math.e)
BIG = 1e30
f32 = jnp.float32
bf16 = jnp.bfloat16

NT = (((1,), (1,)), ((), ()))
NN = (((1,), (0,)), ((), ()))
TN = (((0,), (0,)), ((), ()))


def dot(a, b, dims):
    return lax.dot_general(a, b, dims, preferred_element_type=f32)


def add(*parts):
    total = parts[0].astype(f32)
    for part in parts[1:]:
        total = total + part.astype(f32)
    return total.astype(bf16)


def place():
    x = lax.axis_index("heads")
    ctx = lax.axis_index("ctx")
    return x, ctx // 8, lax.rem(ctx // 2, 4), lax.rem(ctx, 2)


def ctx_id(y, z, core):
    return (y * 4 + z) * 2 + core


def remote(src, dst, send, recv, device):
    return pltpu.make_async_remote_copy(
        src_ref=src, dst_ref=dst, send_sem=send, recv_sem=recv, device_id=device, device_id_type=MESH
    )


def meet():
    x, me = lax.axis_index("heads"), lax.axis_index("ctx")
    barrier = pltpu.get_barrier_semaphore()
    for d in (1, 2, 3):
        pl.semaphore_signal(barrier, inc=1, device_id={"heads": lax.rem(x + d, 4)}, device_id_type=MESH)

    def greet(d, carry):
        pl.semaphore_signal(barrier, inc=1, device_id={"ctx": lax.rem(me + d, NBLK)}, device_id_type=MESH)
        return carry

    lax.fori_loop(1, NBLK, greet, 0)
    pl.semaphore_wait(barrier, NBLK - 1 + 3)


class Ring:
    def __init__(self, batch, half):
        x, y, z, core = place()
        self.half, self.core = half, core
        self.cols = pl.ds(batch * HALF + half * QUARTER, QUARTER)
        self.heads = range((2 * batch + half) * 2, (2 * batch + half + 1) * 2)
        self.a, self.b = (y, z) if half == 0 else (z, y)
        self.side = 1 - 2 * core

    def at_a(self, d):
        return lax.rem(self.a + d + 4, 4)

    def at_b(self, d):
        return lax.rem(self.b + d + 4, 4)

    def device(self, da, db):
        a, b = self.at_a(da), self.at_b(db)
        y, z = (a, b) if self.half == 0 else (b, a)
        return {"ctx": ctx_id(y, z, self.core)}

    def sibling(self):
        y, z = (self.a, self.b) if self.half == 0 else (self.b, self.a)
        return {"ctx": ctx_id(y, z, 1 - self.core)}

    def block(self, ref, a):
        y, z = (a, self.b) if self.half == 0 else (self.b, a)
        return ref.at[y, z, self.core, :, self.cols]

    def line(self, ref, b, core):
        return ref.at[:, b, core, :, self.cols] if self.half == 0 else ref.at[b, :, core, :, self.cols]

    def bare_line(self, ref, b):
        return ref.at[:, b, :, self.cols] if self.half == 0 else ref.at[b, :, :, self.cols]


def settle(send=None, recv=None):
    sem, ref = send or recv
    copy = remote(ref, ref, sem, sem, {"heads": lax.rem(lax.axis_index("heads") + 1, 4)})
    if send:
        copy.wait_send()
    else:
        copy.wait_recv()


class Mover:
    def __init__(self, batch, send, recv):
        self.send, self.recv = send, recv.at[batch]
        self.rings = [Ring(batch, 0), Ring(batch, 1)]

    def go(self, kind, n, src, dst, device):
        remote(src, dst, self.send.at[kind], self.recv.at[n], device).start()


def flush(send, windows):
    settle(send=(send.at[0], windows.at[pl.ds(0, 3), :, :, :, pl.ds(0, QUARTER)]))
    settle(send=(send.at[1], windows.at[pl.ds(0, 3)]))
    settle(send=(send.at[2], windows))


class Gather(Mover):
    def __init__(self, batch, out, send, recv):
        super().__init__(batch, send, recv)
        self.out = out

    def got(self, n, *index):
        settle(recv=(self.recv.at[n], self.out.at[(*index, slice(None), pl.ds(0, QUARTER))]))

    def a_send(self):
        for g in self.rings:
            own = g.block(self.out, g.a)
            for d in (1, 3, 2):
                self.go(0, 4, own, own, g.device(d, 0))

    def to_sibling(self, d):
        for g in self.rings:
            line = g.line(self.out, g.at_b(-d), g.core)
            self.go(2, d, line, line, g.sibling())

    def b_send(self):
        self.got(4, pl.ds(0, 3), 0, slice(None))
        for g in self.rings:
            own = g.line(self.out, g.b, g.core)
            for d in (1, 3):
                self.go(1, 5, own, own, g.device(0, d))
        self.to_sibling(0)

    def near(self):
        self.got(5, slice(None), slice(None), 0)
        for g in self.rings:
            line = g.line(self.out, g.at_b(-g.side), g.core)
            self.go(1, 6, line, line, g.device(0, g.side))
        self.to_sibling(1)
        self.to_sibling(3)

    def far(self):
        self.got(6, slice(None), 0, slice(None))
        self.to_sibling(2)

    def from_sibling(self, d):
        self.got(d, slice(None), 0, slice(None))


class Scatter(Mover):
    def __init__(self, batch, terms, sib, lines, blocks, send, recv):
        super().__init__(batch, send, recv)
        self.terms, self.sib, self.lines, self.blocks = terms, sib, lines.at[batch], blocks.at[batch]

    def to_sibling(self, h, d):
        g = self.rings[h]
        b = g.at_b(d)
        self.go(2, d, g.line(self.terms, b, 1 - g.core), g.bare_line(self.sib, b), g.sibling())

    def from_sibling(self, d):
        settle(recv=(self.recv.at[d], self.sib.at[pl.ds(0, 2), :, :, pl.ds(0, QUARTER)]))

    def b_send(self, d):
        self.from_sibling(d)
        for h, g in enumerate(self.rings):
            b = g.at_b(d)
            mine, other = g.line(self.terms, b, g.core), g.bare_line(self.sib, b)
            mine[...] = mine[...] + other[...]
            self.go(1, 4, mine, self.lines.at[h, d - 1], g.device(0, d))

    def a_send(self):
        self.from_sibling(0)
        settle(recv=(self.recv.at[4], self.lines))
        for h, g in enumerate(self.rings):
            mine, other = g.line(self.terms, g.b, g.core), g.bare_line(self.sib, g.b)
            mine[...] = add(mine[...], other[...], *(self.lines[h, d] for d in range(3)))
            for d in (2, 1, 3):
                self.go(0, 5, g.block(self.terms, g.at_a(d)), self.blocks.at[h, d - 1], g.device(d, 0))

    def finish(self):
        settle(recv=(self.recv.at[5], self.blocks))
        for h, g in enumerate(self.rings):
            mine = g.block(self.terms, g.a)
            mine[...] = add(mine[...], *(self.blocks[h, d] for d in range(3)))


class Heads:
    def __init__(self, wide, own, inward, sems):
        x = lax.axis_index("heads")
        self.send, self.recv, local = (sems.at[n] for n in range(3))
        self.dst = own.at[pl.ds(0, 48), :] if inward else wide.at[:, pl.ds(0, 3 * WIDTH)]

        def cols(x):
            return wide.at[:, pl.ds(pl.multiple_of(x * WIDTH, WIDTH), WIDTH)]

        def rows(x):
            return own.at[pl.ds(pl.multiple_of(x * 16, 16), 16), :]

        for d in (1, 2, 3):
            to = lax.rem(x + d, 4)
            src, dst = (cols(to), rows(x)) if inward else (rows(to), cols(x))
            remote(src, dst, self.send, self.recv, {"heads": to}).start()
        src, dst = (cols(x), rows(x)) if inward else (rows(x), cols(x))
        self.local = pltpu.make_async_copy(src, dst, local)
        self.local.start()

    def arrived(self):
        self.local.wait()
        settle(recv=(self.recv, self.dst))

    def flush(self):
        settle(send=(self.send, self.dst))


def all_lanes(shape):
    return lax.broadcasted_iota(jnp.int32, shape, 1)


def fetch(ref, half, b, h):
    cols = pl.ds(h * DH, DH)
    tile = ref[:, b, :, :, cols] if half == 0 else ref[b, :, :, :, cols]
    return tile.reshape(LINE, DH)


def put(ref, half, b, h, tile):
    tile = tile.reshape(4, 2, ROWS, DH)
    cols = pl.ds(h * DH, DH)
    if half == 0:
        ref[:, b, :, :, cols] = tile
    else:
        ref[b, :, :, :, cols] = tile


def forward_line(ring, d, q, k, vx, weights, out, peaks, bias, first):
    half, b = ring.half, ring.at_b(-d)
    lane = all_lanes((LINE, DH))
    stats = jnp.zeros((LINE, DH), f32) if first else peaks[half, b]
    for h in ring.heads:
        scores = dot(fetch(q, half, b, h), k[:, h * DH : (h + 1) * DH], NT)
        if d == 0:
            late = scores[:, BLOCK - DH :] + bias[half]
            scores = jnp.concatenate([scores[:, : BLOCK - DH], late], axis=1)
        peak = jnp.max(scores, axis=1, keepdims=True)
        w = jnp.exp2((scores - peak) * SCALE2).astype(bf16)
        weights[h, b] = w
        both = dot(w, vx[h], NN)
        put(out, half, b, h, both[:, :DH].astype(bf16))
        stats = jnp.where(lane == h, peak * SCALE, stats)
        stats = jnp.where(lane == HEADS_DEV + h, both[:, DH:], stats)
    peaks[half, b] = stats


def scale_line(ring, d, factors, out):
    half, b = ring.half, ring.at_b(d)
    factor = (factors[:, b] if half == 0 else factors[b]).reshape(LINE, DH)
    for h in ring.heads:
        put(out, half, b, h, (fetch(out, half, b, h).astype(f32) * factor[:, h : h + 1]).astype(bf16))


def backward_line(ring, d, q, g, k, v, weights, factors, out, dq, dk, dv):
    half, b = ring.half, ring.at_b(d)
    factor = (factors[:, b] if half == 0 else factors[b]).reshape(LINE, DH)
    for h in ring.heads:
        cols = slice(h * DH, (h + 1) * DH)
        share, delta = factor[:, h : h + 1], factor[:, HEADS_DEV + h : HEADS_DEV + h + 1]
        grad = (fetch(g, half, b, h).astype(f32) * share).astype(bf16)
        if out is not None:
            put(out, half, b, h, (fetch(out, half, b, h).astype(f32) * share).astype(bf16))
        w = weights[h, b]
        dprob = dot(grad, v[:, cols], NT)
        dscores = (w.astype(f32) * (dprob - delta)).astype(bf16)
        dv[h] += dot(grad, w, TN)
        dk[h] += dot(fetch(q, half, b, h), dscores, TN)
        put(dq, half, b, h, (dot(dscores, k[:, cols], NN) * SCALE).astype(bf16))


def kernel(
    q_in, k_in, v_in, picks_in, g_in,
    out_ref, dq_ref, dk_ref, dv_ref,
    q, g, out, dq, k, v, picks, vx, weights, dk, dv, bias, live, peaks, own_peaks, factors, pick_head,
    tell, told, merged,
    sib, lines, blocks,
    gather_send, gather_recv, scatter_send, scatter_recv,
    heads_sems, stat_send, stat_recv, local,
):
    x, y, z, core = place()
    me = lax.axis_index("ctx")
    out_ref, dq_ref, dk_ref, dv_ref = out_ref.at[0], dq_ref.at[0], dk_ref.at[0], dv_ref.at[0]
    loads = [pltpu.make_async_copy(a, b, local.at[i]) for i, (a, b) in enumerate([(k_in, k), (v_in, v), (picks_in, picks)])]
    for load in loads:
        load.start()
    meet()
    in_q = Heads(q_in, q.at[y, z, core], True, heads_sems.at[0])
    in_g = Heads(g_in, g.at[y, z, core], True, heads_sems.at[1])
    move_q = [Gather(p, q, gather_send, gather_recv.at[0]) for p in (0, 1)]
    move_g = [Gather(p, g, gather_send, gather_recv.at[1]) for p in (0, 1)]
    sum_out, sum_dq = (
        [
            Scatter(p, terms, sib.at[n], lines.at[n], blocks.at[n], scatter_send, scatter_recv.at[n])
            for p in (0, 1)
        ]
        for n, terms in enumerate((out, dq))
    )
    rings = [move_q[p].rings for p in (0, 1)]
    lane = all_lanes((HEADS_DEV, DH))

    def forward(p, d):
        for ring in rings[p]:
            forward_line(ring, d, q, k, vx, weights, out, peaks, bias, p == 0)

    def tell_levels(p):
        active = lax.broadcasted_iota(jnp.int32, (HEADS_DEV, DH), 0) // 4 == p

        def tell_chip(i, carry):
            cy, cz = i // 4, lax.rem(i, 4)
            stats = peaks[0, cz, pl.ds(pl.multiple_of(cy * 2 * ROWS, 2 * ROWS), 2 * ROWS), :]
            stats = stats + peaks[1, cy, pl.ds(pl.multiple_of(cz * 2 * ROWS, 2 * ROWS), 2 * ROWS), :]
            cols = pl.ds(p * HALF, HALF)
            products = (g[cy, cz, :, :, cols].astype(f32) * out[cy, cz, :, :, cols].astype(f32)).reshape(2 * ROWS, HALF)
            high = products.astype(bf16)
            low = (products - high.astype(f32)).astype(bf16)
            turned = (stats + dot(high, pick_head[p], NN) + dot(low, pick_head[p], NN)).T
            total = jnp.where(active, turned[HEADS_DEV : 2 * HEADS_DEV], 1.0)
            peak = turned[:HEADS_DEV] + jnp.where(lane < ROWS, live[2 * i], live[2 * i + 1])
            own_peaks[p, i] = peak
            level = peak + jnp.log(total)
            delta = turned[2 * HEADS_DEV : 3 * HEADS_DEV] / total
            tell[p, 2 * i] = jnp.where(lane < ROWS, level, pltpu.roll(delta, ROWS, 1))
            tell[p, 2 * i + 1] = jnp.where(lane < ROWS, pltpu.roll(level, ROWS, 1), delta)
            return carry

        lax.fori_loop(0, NBLK // 2, tell_chip, 0, unroll=4)

        def send_level(d, carry):
            peer = lax.rem(me + d, NBLK)
            remote(tell.at[p, peer], told.at[p, me], stat_send.at[p, 0], stat_recv.at[p, 0], {"ctx": peer}).start()
            return carry

        lax.fori_loop(1, NBLK, send_level, 0)
        told[p, me] = tell[p, me]

    def hear(p, phase, ref):
        settle(recv=(stat_recv.at[p, phase], ref.at[p, pl.ds(0, NBLK - 1)]))

    def merge_levels(p):
        hear(p, 0, told)
        every = told[p]
        highest = jnp.max(every, axis=0)
        grown = jnp.exp(every - highest[None])
        total = jnp.sum(grown, axis=0)
        level = highest + jnp.log(total)
        delta = jnp.zeros((HEADS_DEV, DH), f32)
        for b in range(NBLK):
            delta = delta + pltpu.roll(grown[b], ROWS, 1) * every[b]
        delta = delta / pltpu.roll(total, ROWS, 1)
        merged[p, me] = jnp.where(lane < ROWS, level, delta)
        mine = merged.at[p, me]

        def share_level(d, carry):
            peer = lax.rem(me + d, NBLK)
            remote(mine, mine, stat_send.at[p, 1], stat_recv.at[p, 1], {"ctx": peer}).start()
            return carry

        lax.fori_loop(1, NBLK, share_level, 0)

    def weigh(p):
        hear(p, 1, merged)

        def weigh_chip(i, carry):
            first, second = merged[p, 2 * i], merged[p, 2 * i + 1]
            level = jnp.where(lane < ROWS, first, pltpu.roll(second, ROWS, 1))
            delta = jnp.where(lane < ROWS, pltpu.roll(first, ROWS, 1), second)
            share = jnp.exp(own_peaks[p, i] - level)
            rows = jnp.concatenate([share, share * delta], axis=0)
            factors[p, i // 4, lax.rem(i, 4), :, : 2 * HEADS_DEV] = rows.T
            return carry

        lax.fori_loop(0, NBLK // 2, weigh_chip, 0, unroll=4)

    def backward(p, d, scale=True, between=None):
        for half, ring in enumerate(rings[p]):
            backward_line(ring, d, q, g, k, v, weights, factors.at[p], out if scale else None, dq, dk, dv)
            if scale:
                sum_out[p].to_sibling(half, d)
            sum_dq[p].to_sibling(half, d)
            if half == 0 and between:
                between()

    def scale(p, d):
        for half, ring in enumerate(rings[p]):
            scale_line(ring, d, factors.at[p], out)
            sum_out[p].to_sibling(half, d)

    def b_send(p, d):
        sum_out[p].b_send(d)
        sum_dq[p].b_send(d)

    saves = []

    def save(p):
        for h in range(4 * p, 4 * p + 4):
            cols = slice(h * DH, (h + 1) * DH)
            k[:, cols] = (dk[h] * SCALE).T.astype(bf16)
            v[:, cols] = dv[h].T.astype(bf16)
        cols = pl.ds(p * HALF, HALF)
        for n, (src, dst) in enumerate([(k, dk_ref), (v, dv_ref)]):
            saves.append(pltpu.make_async_copy(src.at[:, cols], dst.at[:, cols], local.at[2 * p + n]))
            saves[-1].start()

    for load in loads:
        load.wait()
    for h in range(HEADS_DEV):
        vx[h, :, :DH] = v[:, h * DH : (h + 1) * DH]
        vx[h, :, DH:] = jnp.ones((BLOCK, DH), bf16)
    in_q.arrived()
    move_q[0].a_send()
    in_g.arrived()
    move_g[0].a_send()
    move_q[0].b_send()
    move_q[1].a_send()
    bias[...] = jnp.zeros_like(bias)
    row = lax.broadcasted_iota(jnp.int32, (ROWS, DH), 0)
    late = jnp.where(all_lanes((ROWS, DH)) - (DH - ROWS) > row, -BIG, 0.0)
    for half, r in enumerate(rings[0]):
        bias[half, pl.ds(pl.multiple_of((r.a * 2 + core) * ROWS, ROWS), ROWS), :] = late
    col = lax.broadcasted_iota(jnp.int32, (HALF, DH), 0) // DH
    for p in (0, 1):
        pick_head[p] = jnp.where(all_lanes((HALF, DH)) == col + 2 * HEADS_DEV + 4 * p, 1.0, 0.0).astype(bf16)
    dk[...] = jnp.zeros_like(dk)
    dv[...] = jnp.zeros_like(dv)
    chosen = jnp.max(jnp.where(picks[...] == me, 0.0, -BIG), axis=0, keepdims=True)
    for b in range(NBLK):
        live[b] = jnp.broadcast_to(chosen[:, b : b + 1], (HEADS_DEV, DH))

    move_g[0].b_send()
    move_g[1].a_send()
    move_q[0].from_sibling(0)
    forward(0, 0)
    move_q[0].near()
    move_g[0].near()
    move_q[1].b_send()
    move_q[0].from_sibling(1)
    forward(0, 1)
    move_g[1].b_send()
    move_q[0].from_sibling(3)
    forward(0, 3)
    move_q[0].far()
    move_g[0].far()
    move_q[1].from_sibling(0)
    forward(1, 0)
    move_q[0].from_sibling(2)
    forward(0, 2)
    move_q[1].near()
    for d in (0, 1, 3, 2):
        move_g[0].from_sibling(d)
    tell_levels(0)
    move_g[1].near()
    move_q[1].from_sibling(1)
    forward(1, 1)
    move_q[1].far()
    move_g[1].far()
    move_q[1].from_sibling(3)
    forward(1, 3)
    merge_levels(0)
    move_q[1].from_sibling(2)
    forward(1, 2)
    for d in (0, 1, 3, 2):
        move_g[1].from_sibling(d)
    tell_levels(1)
    weigh(0)

    backward(0, 2)
    merge_levels(1)
    backward(0, 1, between=lambda: b_send(0, 2))
    backward(0, 3, between=lambda: b_send(0, 1))
    weigh(1)
    scale(1, 3)
    b_send(0, 3)
    scale(1, 1)
    backward(1, 2, between=lambda: sum_out[1].b_send(3))
    sum_out[1].b_send(1)
    backward(1, 1, scale=False, between=lambda: b_send(1, 2))
    backward(1, 3, scale=False, between=lambda: sum_dq[1].b_send(1))
    scale(0, 0)
    scale(1, 0)
    sum_dq[1].b_send(3)
    backward(0, 0, scale=False, between=sum_out[0].a_send)
    sum_dq[0].a_send()
    backward(1, 0, scale=False, between=sum_out[1].a_send)
    save(0)
    sum_dq[1].a_send()
    sum_out[0].finish()
    sum_out[1].finish()
    out_heads = Heads(out_ref, out.at[y, z, core], False, heads_sems.at[2])
    sum_dq[0].finish()
    save(1)
    sum_dq[1].finish()
    dq_heads = Heads(dq_ref, dq.at[y, z, core], False, heads_sems.at[3])
    out_heads.arrived()
    for p in (0, 1):
        for phase in (0, 1):
            settle(send=(stat_send.at[p, phase], tell.at[p, pl.ds(0, NBLK - 1)]))
    flush(gather_send, q)
    flush(scatter_send, q)
    for heads in (in_q, in_g, out_heads):
        heads.flush()
    for copy in saves:
        copy.wait()
    dq_heads.arrived()
    dq_heads.flush()


def hand_out(*refs):
    given, taken, held, (arrive, leave) = refs[:4], refs[4:8], refs[8:12], refs[12:]
    pieces = [(i, pl.ds(n * DH, DH)) for n in range(BLOCK // DH) for i in (2, 3)] + [(i, slice(None)) for i in (0, 1)]
    loads, stores = [], []
    for n, (i, rows) in enumerate(pieces):
        loads.append(pltpu.make_async_copy(given[i].at[:, rows], held[i].at[:, rows], arrive.at[n]))
        stores.append(pltpu.make_async_copy(held[i].at[:, rows], taken[i].at[:, rows], leave.at[n]))
    for load in loads:
        load.start()
    for load, store in zip(loads, stores):
        load.wait()
        store.start()
    for store in stores:
        store.wait()


def body(queries, keys, values, picks, d_out):
    rows, wide = jax.ShapeDtypeStruct((1, 16, 4 * WIDTH), bf16), jax.ShapeDtypeStruct((1, BLOCK, WIDTH), bf16)
    anywhere = pl.BlockSpec(memory_space=pl.ANY)
    windows = pltpu.VMEM((4, 4, 2, ROWS, WIDTH), bf16)
    levels = pltpu.VMEM((2, NBLK, HEADS_DEV, DH), f32)
    dma = pltpu.SemaphoreType.DMA
    out, dq, dk, dv = pl.pallas_call(
        kernel,
        out_shape=(rows, rows, wide, wide),
        in_specs=[anywhere] * 5,
        out_specs=[anywhere] * 4,
        scratch_shapes=[
            windows, windows, windows, windows,
            pltpu.VMEM((BLOCK, WIDTH), bf16), pltpu.VMEM((BLOCK, WIDTH), bf16),
            pltpu.VMEM(picks.shape[::-1], jnp.int32),
            pltpu.VMEM((HEADS_DEV, BLOCK, 2 * DH), bf16),
            pltpu.VMEM((HEADS_DEV, 4, LINE, BLOCK), bf16),
            pltpu.VMEM((HEADS_DEV, DH, BLOCK), f32), pltpu.VMEM((HEADS_DEV, DH, BLOCK), f32),
            pltpu.VMEM((2, LINE, DH), f32),
            pltpu.VMEM((NBLK, HEADS_DEV, DH), f32),
            pltpu.VMEM((2, 4, LINE, DH), f32),
            pltpu.VMEM((2, NBLK // 2, HEADS_DEV, DH), f32), pltpu.VMEM((2, 4, 4, 2 * ROWS, DH), f32),
            pltpu.VMEM((2, HALF, DH), bf16),
            levels, levels, levels,
            pltpu.VMEM((2, 4, 4, ROWS, WIDTH), bf16),
            pltpu.VMEM((2, 2, 2, 3, 4, ROWS, QUARTER), bf16), pltpu.VMEM((2, 2, 2, 3, ROWS, QUARTER), bf16),
            dma((3,)), dma((2, 2, 7)), dma((3,)), dma((2, 2, 6)),
            dma((4, 3)), dma((2, 2)), dma((2, 2)), dma((4,)),
        ],
        compiler_params=pltpu.CompilerParams(collective_id=0, has_side_effects=True, vmem_limit_bytes=63 << 20),
        name="block_attention",
    )(queries[0], keys[0], values[0], picks.T, d_out[0])
    return pl.pallas_call(
        hand_out,
        out_shape=(out, dq, dk, dv),
        in_specs=[anywhere] * 4,
        out_specs=[anywhere] * 4,
        scratch_shapes=[pltpu.VMEM(a.shape, bf16) for a in (out, dq, dk, dv)] + [dma((10,)), dma((10,))],
        compiler_params=pltpu.CompilerParams(vmem_limit_bytes=63 << 20),
        name="hand_out",
    )(out, dq, dk, dv)


def solution(mesh):
    rows, blocks = P("ctx", "heads", None), P("ctx", None, "heads")
    return jax.shard_map(
        body,
        mesh=mesh,
        in_specs=(rows, blocks, blocks, P(), rows),
        out_specs=(rows, rows, blocks, blocks),
        check_vma=False,
    )
```
